32 devices in a mesh: dp: 8 (over y, x, core), fsdp: 4 (over z).
Axes of the slice: x: 2, y: 2, z: 4, core: 2. Of those that a mesh axis runs over, the one named last changes fastest.
Arguments:
- activations: bfloat16 [2048, 4096], P('dp', 'fsdp'), may hold values from -6 to 6
- output_grads: bfloat16 [2048, 4096], P('dp', 'fsdp'), may hold values from -6 to 6
- basis: bfloat16 [4096, 1024], P('fsdp'), may hold values from -0.09375 to 0.09375
- weight: bfloat16 [4096, 4096], P('fsdp'), may hold values from -0.09375 to 0.09375
- first_moment: float32 [4096, 1024], P(('fsdp', 'dp')), may hold values from -0.06 to 0.06
- second_moment: float32 [4096, 1024], P(('fsdp', 'dp')), may hold values from 1e-07 to 1e-05
Outputs:
- new_weight: bfloat16 [4096, 4096], P('fsdp')
- new_first: float32 [4096, 1024], P(('fsdp', 'dp'))
- new_second: float32 [4096, 1024], P(('fsdp', 'dp'))
The draws below stay inside these ranges and needn't reach their ends.
All inputs are finite; a program needn't handle non-finite values.
Results may differ from the reference program's by a relative error of at most 0.0036.
Values may be sent and summed in bfloat16 or wider, within the bound.
A program may use at most 64 MiB of HBM per device.

```python
import math
import jax
import jax.numpy as jnp
from jax import lax

D = 4096
RANK = 1024
TOKENS = 2048


def with_spikes(result, key, source, target, shards_of, factor):
    def block_of(dim):
        return (jnp.arange(result.shape[dim]) // (result.shape[dim] // shards_of)).reshape((-1,) + (1,) * (result.ndim - 1 - dim))

    first = jax.random.permutation(key, shards_of)[block_of(target)]
    other_side = (block_of(target) + shards_of // 2) % shards_of
    return jnp.where((block_of(source) == first) | (block_of(source) == other_side), factor * result, result)


def shard_levels(stream_key, extent, shards, low, high):
    def one(position, blocks):
        draws = jax.random.uniform(jax.random.fold_in(jax.random.fold_in(stream_key, 6), position), (blocks,), jnp.float32, low / len(shards), high / len(shards))
        return jnp.repeat(jnp.exp(draws), extent[position] // blocks).reshape((-1,) + (1,) * (len(extent) - position - 1))

    gain = one(*shards[0])
    for cut in shards[1:]:
        gain = gain * one(*cut)
    return gain


def noise(rng, shape, spread, reach, split=(), dtype=jnp.bfloat16):
    array = jax.random.normal(rng, shape, jnp.float32) * spread
    if len(split) > 0:
        array = shard_levels(rng, shape, split, -0.22, 0.18) * array
    return jnp.clip(array, min=-reach, max=reach).astype(dtype)


def bell_draw_with(stream_key, extent, spread, bound, split, heavy, kind=jnp.bfloat16):
    drawn = spread * jax.random.normal(stream_key, extent, jnp.float32)
    if split:
        drawn = drawn * shard_levels(stream_key, extent, split, -0.22, 0.18)
    return jnp.clip(with_spikes(drawn, jax.random.fold_in(stream_key, 3), *heavy), -bound, bound).astype(kind)


def setup_inputs(seed: int = 0) -> dict:
    seeds = jax.random.split(jax.random.key(seed), 7)
    activations = noise(seeds[0], (TOKENS, D), 1.0, 6.0, ((0, 8), (1, 4)))
    output_grads = bell_draw_with(seeds[1], (TOKENS, D), 1.0, 6.0, ((0, 8), (1, 4)), (0, 1, 8, 2.0))
    basis = noise(seeds[2], (D, RANK), D ** -0.5, 0.09375, ((0, 4),))
    weight = noise(seeds[3], (D, D), D ** -0.5, 0.09375, ((0, 4),))
    first_moment = noise(seeds[4], (D, RANK), 0.01, 0.06, ((0, 32),), jnp.float32)
    second_moment = jnp.clip(jnp.exp(math.log(9.999999747378752e-06) - 4.6051701 * jax.random.uniform(seeds[5], (D, RANK), jnp.float32) ** shard_levels(seeds[5], (D, RANK), ((0, 32),), -0.2, 0.2)), 1.0000000116860974e-07, 9.999999747378752e-06)
    return dict(activations=activations, output_grads=output_grads, basis=basis, weight=weight, first_moment=first_moment, second_moment=second_moment)


first_decay = 0.9
second_decay = 0.999
first_fix = 1.0 - 0.9 ** 10
second_fix = 1.0 - 0.999 ** 10
step_rate = 0.01
tiny_eps = 1e-08

def reference(activations, output_grads, basis, weight, first_moment, second_moment):
    projected = jnp.dot(activations, basis, preferred_element_type=jnp.float32).astype(jnp.bfloat16)
    low_grad = lax.dot_general(output_grads, projected, (((0,), (0,)), ((), ())), preferred_element_type=jnp.float32) / TOKENS
    new_first = first_decay * first_moment + (1.0 - first_decay) * low_grad
    new_second = second_decay * second_moment + (1.0 - second_decay) * low_grad * low_grad
    update = (new_first / first_fix / (jnp.sqrt(new_second / second_fix) + tiny_eps)).astype(jnp.bfloat16)
    decoded = lax.dot_general(update, basis, (((1,), (1,)), ((), ())), preferred_element_type=jnp.float32)
    new_weight = (weight.astype(jnp.float32) - step_rate * decoded).astype(jnp.bfloat16)
    return (new_weight, new_first, new_second)
```

```python
import functools

import jax
import jax.numpy as jnp
from jax import lax
from jax.experimental import pallas as pl
from jax.experimental.pallas import tpu as pltpu
from jax.sharding import PartitionSpec as P

first_decay = 0.9
second_decay = 0.999
first_fix = 1.0 - 0.9**10
second_fix = 1.0 - 0.999**10
step_rate = 0.01
tiny_eps = 1e-08
MESH = pl.DeviceIdType.MESH
f32 = jnp.float32
bf16 = jnp.bfloat16


def times_basis(update, rows):
    return lax.dot_general(update, rows, (((1,), (1,)), ((), ())), preferred_element_type=f32)


def adam(first, second, low_grad):
    new_first = first_decay * first + (1.0 - first_decay) * low_grad
    new_second = second_decay * second + (1.0 - second_decay) * low_grad * low_grad
    update = (new_first / first_fix / (jnp.sqrt(new_second / second_fix) + tiny_eps)).astype(bf16)
    return new_first, new_second, update


def exchange_kernel(
    act, og, basis, first, second,
    updates, rows_out, new_first, new_second,
    part, part_send, part_recv, proj,
    grad, grad_core, sa1, sb1, ra1, rb1, sa2, sb2, ra2, rb2,
    own_sem, z_send, z_fwd, z_recv, rs_send, rs_recv, ag_send, ag_recv,
    core_send, core_recv, h1_send, h1_recv, h2_send, h2_recv, pg_send, pg_recv,
):
    i = lax.axis_index("dp")
    j = lax.axis_index("fsdp")
    ndp, nf = 8, 4
    core, x, y = i % 2, (i // 2) % 2, i // 4
    sib = i + 1 - 2 * core
    xn = i + 2 * (1 - 2 * x)
    yn = i + 4 * (1 - 2 * y)
    dn = xn + 4 * (1 - 2 * y)
    tokens, rank = act.shape[0], first.shape[1]
    own_rows = first.shape[0]
    tb = tokens // nf
    half = rank // 2
    total_tokens = tokens * ndp

    def remote(src, dst, ssem, rsem, dp, z):
        return pltpu.make_async_remote_copy(
            src_ref=src, dst_ref=dst, send_sem=ssem, recv_sem=rsem,
            device_id=(dp, z), device_id_type=MESH,
        )

    def got(dst, rsem, ssem):
        remote(dst, dst, ssem, rsem, sib, j).wait_recv()

    def sent(src, ssem, rsem):
        remote(src, src, ssem, rsem, sib, j).wait_send()

    barrier = pltpu.get_barrier_semaphore()
    for dp in (sib, xn, yn):
        pl.semaphore_signal(barrier, inc=1, device_id=(dp, j), device_id_type=MESH)
    for d in range(1, nf):
        pl.semaphore_signal(barrier, inc=1, device_id=(i, (j + d) % nf), device_id_type=MESH)
    pl.semaphore_wait(barrier, 3 + nf - 1)

    own_copy = pltpu.make_async_copy(basis, rows_out.at[pl.ds(j * ndp, ndp)], own_sem)
    own_copy.start()

    def z_piece(shard):
        return rows_out.at[shard * ndp + i]

    @pl.when(j < nf - 1)
    def _():
        remote(basis.at[i], z_piece(j), z_send.at[0], z_recv.at[j], i, j + 1).start()

    @pl.when(j > 0)
    def _():
        remote(basis.at[i], z_piece(j), z_send.at[1], z_recv.at[j], i, j - 1).start()

    a = act[...]
    acc = None
    for k in range(ndp):
        term = jnp.dot(a[:, k * own_rows : (k + 1) * own_rows], basis[k], preferred_element_type=f32)
        acc = term if acc is None else acc + term
    part[...] = acc.reshape(nf, tb, rank)
    part_send[...] = acc.reshape(nf, tb, rank).astype(bf16)
    for d in (1, 2, 3):
        z = (j + d) % nf
        remote(part_send.at[z], part_recv.at[j], rs_send.at[z], rs_recv.at[j], i, z).start()

    def block(buf, base, k):
        return buf.at[base + k]

    def lane_a(buf, base, k):
        return buf.at[base + k, :, pl.ds(0, half)]

    def lane_b(buf, base, k):
        return buf.at[base + k, :, pl.ds(half, half)]

    def stage1(buf, base, g):
        mine = block(buf, base, i)
        remote(mine, mine, pg_send.at[g, 0], pg_recv.at[g, 0], xn, j).start()
        remote(mine, mine, pg_send.at[g, 1], pg_recv.at[g, 1], yn, j).start()
        remote(mine, mine, pg_send.at[g, 4], pg_recv.at[g, 4], sib, j).start()

    def stage2(buf, base, g):
        bx, by = block(buf, base, xn), block(buf, base, yn)
        got(bx, pg_recv.at[g, 0], pg_send.at[g, 0])
        lb = lane_b(buf, base, xn)
        remote(lb, lb, pg_send.at[g, 3], pg_recv.at[g, 3], yn, j).start()
        remote(bx, bx, pg_send.at[g, 5], pg_recv.at[g, 5], sib, j).start()
        got(by, pg_recv.at[g, 1], pg_send.at[g, 1])
        la = lane_a(buf, base, yn)
        remote(la, la, pg_send.at[g, 2], pg_recv.at[g, 2], xn, j).start()
        remote(by, by, pg_send.at[g, 6], pg_recv.at[g, 6], sib, j).start()

    def stage3(buf, base, g):
        got(lane_a(buf, base, dn), pg_recv.at[g, 2], pg_send.at[g, 2])
        got(lane_b(buf, base, dn), pg_recv.at[g, 3], pg_send.at[g, 3])
        bd = block(buf, base, dn)
        remote(bd, bd, pg_send.at[g, 7], pg_recv.at[g, 7], sib, j).start()

    def stage4(buf, base, g):
        for q in range(4):
            o = (i, xn, yn, dn)[q]
            so = o + 1 - 2 * core
            got(block(buf, base, so), pg_recv.at[g, 4 + q], pg_send.at[g, 4 + q])
            sent(block(buf, base, o), pg_send.at[g, 4 + q], pg_recv.at[g, 4 + q])
        sent(block(buf, base, i), pg_send.at[g, 0], pg_recv.at[g, 0])
        sent(block(buf, base, i), pg_send.at[g, 1], pg_recv.at[g, 1])
        sent(lane_a(buf, base, yn), pg_send.at[g, 2], pg_recv.at[g, 2])
        sent(lane_b(buf, base, xn), pg_send.at[g, 3], pg_recv.at[g, 3])

    low = 1 - j // 2
    edge = low * j + (1 - low) * (nf - 1 - j)

    def shard_of(g):
        place = g + (g + nf - edge) // nf
        return low * place + (1 - low) * (nf - 1 - place)

    def basis_in(g):
        s = shard_of(g)
        got(z_piece(s), z_recv.at[s], z_send.at[0])

        @pl.when((s < j) & (j < nf - 1))
        def _():
            remote(z_piece(s), z_piece(s), z_fwd.at[g], z_recv.at[s], i, j + 1).start()

        @pl.when((s > j) & (j > 0))
        def _():
            remote(z_piece(s), z_piece(s), z_fwd.at[g], z_recv.at[s], i, j - 1).start()

        stage1(rows_out, s * ndp, g)

    def basis_sent(g):
        s = shard_of(g)

        @pl.when(((s < j) & (j < nf - 1)) | ((s > j) & (j > 0)))
        def _():
            sent(z_piece(s), z_fwd.at[g], z_recv.at[s])

    basis_in(0)

    total = part[j]
    for d in (1, 2, 3):
        z = (j + d) % nf
        got(part_recv.at[z], rs_recv.at[z], rs_send.at[z])
        total = total + part_recv[z].astype(f32)
    proj[j] = total.astype(bf16)
    for d in (1, 2, 3):
        z = (j + d) % nf
        remote(proj.at[j], proj.at[j], ag_send.at[z], ag_recv.at[j], i, z).start()

    basis_in(1)
    stage2(rows_out, shard_of(0) * ndp, 0)

    for d in (1, 2, 3):
        z = (j + d) % nf
        got(proj.at[z], ag_recv.at[z], ag_send.at[z])

    projected = proj[...].reshape(tokens, rank)

    def term(k):
        cols = pl.ds(pl.multiple_of(k * own_rows, own_rows), own_rows)
        return lax.dot_general(
            og[:, cols], projected, (((0,), (0,)), ((), ())), preferred_element_type=f32
        ) / total_tokens

    for q in range(4):
        grad[4 + q] = term(2 * q + 1 - core)
        remote(grad.at[4 + q], grad_core.at[q], core_send.at[q], core_recv.at[q], sib, j).start()
    for q in range(4):
        grad[q] = term(2 * q + core)
    for q in range(4):
        got(grad_core.at[q], core_recv.at[q], core_send.at[q])
        grad[q] = grad[q] + grad_core[q]

    for n, far in enumerate((1, 0)):
        yy = far * (1 - y) + (1 - far) * y
        sa1[n] = grad[2 * yy + 1 - x, :, 0:half].astype(bf16)
        remote(sa1.at[n], ra1.at[n], h1_send.at[n], h1_recv.at[n], xn, j).start()
        xx = far * (1 - x) + (1 - far) * x
        sb1[n] = grad[2 * (1 - y) + xx, :, half:rank].astype(bf16)
        remote(sb1.at[n], rb1.at[n], h1_send.at[2 + n], h1_recv.at[2 + n], yn, j).start()
    got(ra1.at[0], h1_recv.at[0], h1_send.at[0])
    sa2[...] = grad[2 * (1 - y) + x, :, 0:half] + ra1[0].astype(f32)
    remote(sa2, ra2, h2_send.at[0], h2_recv.at[0], yn, j).start()
    got(rb1.at[0], h1_recv.at[2], h1_send.at[2])
    sb2[...] = grad[2 * y + 1 - x, :, half:rank] + rb1[0].astype(f32)
    remote(sb2, rb2, h2_send.at[1], h2_recv.at[1], xn, j).start()
    got(ra1.at[1], h1_recv.at[1], h1_send.at[1])
    got(rb1.at[1], h1_recv.at[3], h1_send.at[3])

    mine = 2 * y + x
    got(ra2, h2_recv.at[0], h2_send.at[0])
    nf_a, ns_a, up_a = adam(
        first[:, 0:half], second[:, 0:half], grad[mine, :, 0:half] + ra1[1].astype(f32) + ra2[...]
    )
    new_first[:, 0:half] = nf_a
    new_second[:, 0:half] = ns_a
    updates[i, :, 0:half] = up_a
    got(rb2, h2_recv.at[1], h2_send.at[1])
    nf_b, ns_b, up_b = adam(
        first[:, half:rank], second[:, half:rank], grad[mine, :, half:rank] + rb1[1].astype(f32) + rb2[...]
    )
    new_first[:, half:rank] = nf_b
    new_second[:, half:rank] = ns_b
    updates[i, :, half:rank] = up_b
    stage1(updates, 0, 3)

    basis_in(2)
    stage2(rows_out, shard_of(1) * ndp, 1)
    stage3(rows_out, shard_of(0) * ndp, 0)
    stage2(updates, 0, 3)
    stage3(rows_out, shard_of(1) * ndp, 1)
    stage2(rows_out, shard_of(2) * ndp, 2)
    stage3(updates, 0, 3)
    stage3(rows_out, shard_of(2) * ndp, 2)
    for g in range(3):
        stage4(rows_out, shard_of(g) * ndp, g)
        basis_sent(g)
    stage4(updates, 0, 3)

    own_copy.wait()

    @pl.when(j < nf - 1)
    def _():
        sent(basis.at[i], z_send.at[0], z_recv.at[j])

    @pl.when(j > 0)
    def _():
        sent(basis.at[i], z_send.at[1], z_recv.at[j])

    for d in (1, 2, 3):
        z = (j + d) % nf
        sent(part_send.at[z], rs_send.at[z], rs_recv.at[z])
        sent(proj.at[j], ag_send.at[z], ag_recv.at[z])
    for q in range(4):
        sent(grad.at[4 + q], core_send.at[q], core_recv.at[q])
    for n in range(2):
        sent(sa1.at[n], h1_send.at[n], h1_recv.at[n])
        sent(sb1.at[n], h1_send.at[2 + n], h1_recv.at[2 + n])
    sent(sa2, h2_send.at[0], h2_recv.at[0])
    sent(sb2, h2_send.at[1], h2_recv.at[1])


def local_fused(activations, output_grads, basis, weight, first_moment, second_moment):
    tokens, _ = activations.shape
    shard_rows, rank = basis.shape
    own_rows = first_moment.shape[0]
    ndp, nf = lax.axis_size("dp"), lax.axis_size("fsdp")
    half = rank // 2
    vmem = pl.BlockSpec(memory_space=pltpu.VMEM)
    dma = pltpu.SemaphoreType.DMA
    updates, rows, new_first, new_second = pl.pallas_call(
        exchange_kernel,
        out_shape=(
            jax.ShapeDtypeStruct((ndp, own_rows, rank), bf16),
            jax.ShapeDtypeStruct((nf * ndp, own_rows, rank), bf16),
            jax.ShapeDtypeStruct((own_rows, rank), f32),
            jax.ShapeDtypeStruct((own_rows, rank), f32),
        ),
        in_specs=[vmem] * 5,
        out_specs=(vmem, pl.BlockSpec(memory_space=pl.ANY), vmem, vmem),
        scratch_shapes=[
            pltpu.VMEM((nf, tokens // nf, rank), f32),
            pltpu.VMEM((nf, tokens // nf, rank), bf16),
            pltpu.VMEM((nf, tokens // nf, rank), bf16),
            pltpu.VMEM((nf, tokens // nf, rank), bf16),
            pltpu.VMEM((ndp, own_rows, rank), f32),
            pltpu.VMEM((ndp // 2, own_rows, rank), f32),
            pltpu.VMEM((2, own_rows, half), bf16),
            pltpu.VMEM((2, own_rows, half), bf16),
            pltpu.VMEM((2, own_rows, half), bf16),
            pltpu.VMEM((2, own_rows, half), bf16),
            pltpu.VMEM((own_rows, half), f32),
            pltpu.VMEM((own_rows, half), f32),
            pltpu.VMEM((own_rows, half), f32),
            pltpu.VMEM((own_rows, half), f32),
            dma, dma((2,)), dma((3,)), dma((nf,)), dma((nf,)), dma((nf,)), dma((nf,)), dma((nf,)),
            dma((4,)), dma((4,)), dma((4,)), dma((4,)), dma((2,)), dma((2,)), dma((4, 8)), dma((4, 8)),
        ],
        compiler_params=pltpu.CompilerParams(
            collective_id=0, has_side_effects=True, vmem_limit_bytes=48 * 1024 * 1024
        ),
        cost_estimate=pl.CostEstimate(
            flops=4 * tokens * shard_rows * rank, bytes_accessed=24 * 1024 * 1024, transcendentals=0
        ),
    )(
        activations, output_grads, basis.reshape(ndp, own_rows, rank), first_moment, second_moment
    )
    decoded = times_basis(updates.reshape(shard_rows, rank), rows.reshape(nf * shard_rows, rank))
    new_weight = (weight.astype(f32) - step_rate * decoded).astype(bf16)
    return (new_weight, new_first, new_second)


def local(activations, output_grads, basis, weight, first_moment, second_moment):
    partial_product = jnp.dot(activations, basis, preferred_element_type=f32)
    projected = lax.psum(partial_product, "fsdp").astype(bf16)
    total_tokens = projected.shape[0] * lax.axis_size("dp")
    local_term = (
        lax.dot_general(
            output_grads, projected, (((0,), (0,)), ((), ())), preferred_element_type=f32
        )
        / total_tokens
    )
    low_grad = lax.psum_scatter(local_term, "dp", scatter_dimension=0, tiled=True)
    new_first, new_second, update = adam(first_moment, second_moment, low_grad)
    all_updates = lax.all_gather(update, "dp", axis=0, tiled=True)
    decoded = times_basis(all_updates, lax.all_gather(basis, "fsdp", axis=0, tiled=True))
    new_weight = (weight.astype(f32) - step_rate * decoded).astype(bf16)
    return (new_weight, new_first, new_second)


def solution(mesh):
    fused = mesh.shape["dp"] == 8 and mesh.shape["fsdp"] == 4
    return jax.shard_map(
        local_fused if fused else local,
        mesh=mesh,
        in_specs=(
            P("dp", "fsdp"),
            P("dp", "fsdp"),
            P("fsdp", None),
            P("fsdp", None),
            P(("fsdp", "dp"), None),
            P(("fsdp", "dp"), None),
        ),
        out_specs=(P("fsdp", None), P(("fsdp", "dp"), None), P(("fsdp", "dp"), None)),
        check_vma=False,
    )
```

```python
import functools

import jax
import jax.numpy as jnp
from jax import lax
from jax.experimental import pallas as pl
from jax.experimental.pallas import tpu as pltpu
from jax.sharding import PartitionSpec as P

first_decay = 0.9
second_decay = 0.999
first_fix = 1.0 - 0.9**10
second_fix = 1.0 - 0.999**10
step_rate = 0.01
tiny_eps = 1e-08
MESH = pl.DeviceIdType.MESH
f32 = jnp.float32
bf16 = jnp.bfloat16


def times_basis(update, rows):
    return lax.dot_general(update, rows, (((1,), (1,)), ((), ())), preferred_element_type=f32)


def adam(first, second, low_grad):
    new_first = first_decay * first + (1.0 - first_decay) * low_grad
    new_second = second_decay * second + (1.0 - second_decay) * low_grad * low_grad
    update = (new_first / first_fix / (jnp.sqrt(new_second / second_fix) + tiny_eps)).astype(bf16)
    return new_first, new_second, update


def fused_kernel(
    act_in, og_in, basis_in_ref, weight_in, first_in, second_in,
    weight_out, first_out, second_out,
    act, og, rows, weight, first, second, updates,
    part, part_send, part_recv, proj,
    grad, grad_core, sa1, sb1, ra1, rb1, sa2, sb2, ra2, rb2,
    load_sem, store_sem, z_send, z_fwd, z_recv, rs_send, rs_recv, ag_send, ag_recv,
    core_send, core_recv, h1_send, h1_recv, h2_send, h2_recv, pg_send, pg_recv,
):
    i = lax.axis_index("dp")
    j = lax.axis_index("fsdp")
    ndp, nf = 8, 4
    core, x, y = i % 2, (i // 2) % 2, i // 4
    sib = i + 1 - 2 * core
    xn = i + 2 * (1 - 2 * x)
    yn = i + 4 * (1 - 2 * y)
    dn = xn + 4 * (1 - 2 * y)
    tokens, rank = act.shape[0], first.shape[1]
    own_rows = first.shape[0]
    tb = tokens // nf
    half = rank // 2
    total_tokens = tokens * ndp

    loads = [
        pltpu.make_async_copy(src, dst, load_sem.at[n])
        for n, (src, dst) in enumerate((
            (act_in, act),
            (basis_in_ref, rows.at[pl.ds(j * ndp, ndp)]),
            (og_in, og),
            (first_in, first),
            (second_in, second),
            (weight_in, weight),
        ))
    ]
    for load in loads:
        load.start()

    def remote(src, dst, ssem, rsem, dp, z):
        return pltpu.make_async_remote_copy(
            src_ref=src, dst_ref=dst, send_sem=ssem, recv_sem=rsem,
            device_id=(dp, z), device_id_type=MESH,
        )

    def got(dst, rsem, ssem):
        remote(dst, dst, ssem, rsem, sib, j).wait_recv()

    def sent(src, ssem, rsem):
        remote(src, src, ssem, rsem, sib, j).wait_send()

    barrier = pltpu.get_barrier_semaphore()
    for dp in (sib, xn, yn):
        pl.semaphore_signal(barrier, inc=1, device_id=(dp, j), device_id_type=MESH)
    for d in range(1, nf):
        pl.semaphore_signal(barrier, inc=1, device_id=(i, (j + d) % nf), device_id_type=MESH)
    pl.semaphore_wait(barrier, 3 + nf - 1)

    def z_piece(shard):
        return rows.at[shard * ndp + i]

    @pl.when(j < nf - 1)
    def _():
        remote(basis_in_ref.at[i], z_piece(j), z_send.at[0], z_recv.at[j], i, j + 1).start()

    @pl.when(j > 0)
    def _():
        remote(basis_in_ref.at[i], z_piece(j), z_send.at[1], z_recv.at[j], i, j - 1).start()

    loads[0].wait()
    loads[1].wait()
    a = act[...]
    acc = None
    for k in range(ndp):
        term = jnp.dot(a[:, k * own_rows : (k + 1) * own_rows], rows[j * ndp + k], preferred_element_type=f32)
        acc = term if acc is None else acc + term
    part[...] = acc.reshape(nf, tb, rank)
    part_send[...] = acc.reshape(nf, tb, rank).astype(bf16)
    for d in (1, 2, 3):
        z = (j + d) % nf
        remote(part_send.at[z], part_recv.at[j], rs_send.at[z], rs_recv.at[j], i, z).start()

    def block(buf, base, k):
        return buf.at[base + k]

    def lane_a(buf, base, k):
        return buf.at[base + k, :, pl.ds(0, half)]

    def lane_b(buf, base, k):
        return buf.at[base + k, :, pl.ds(half, half)]

    def stage1(buf, base, g):
        mine = block(buf, base, i)
        remote(mine, mine, pg_send.at[g, 0], pg_recv.at[g, 0], xn, j).start()
        remote(mine, mine, pg_send.at[g, 1], pg_recv.at[g, 1], yn, j).start()
        remote(mine, mine, pg_send.at[g, 4], pg_recv.at[g, 4], sib, j).start()

    def stage2(buf, base, g):
        bx, by = block(buf, base, xn), block(buf, base, yn)
        got(bx, pg_recv.at[g, 0], pg_send.at[g, 0])
        lb = lane_b(buf, base, xn)
        remote(lb, lb, pg_send.at[g, 3], pg_recv.at[g, 3], yn, j).start()
        remote(bx, bx, pg_send.at[g, 5], pg_recv.at[g, 5], sib, j).start()
        got(by, pg_recv.at[g, 1], pg_send.at[g, 1])
        la = lane_a(buf, base, yn)
        remote(la, la, pg_send.at[g, 2], pg_recv.at[g, 2], xn, j).start()
        remote(by, by, pg_send.at[g, 6], pg_recv.at[g, 6], sib, j).start()

    def stage3(buf, base, g):
        got(lane_a(buf, base, dn), pg_recv.at[g, 2], pg_send.at[g, 2])
        got(lane_b(buf, base, dn), pg_recv.at[g, 3], pg_send.at[g, 3])
        bd = block(buf, base, dn)
        remote(bd, bd, pg_send.at[g, 7], pg_recv.at[g, 7], sib, j).start()

    def stage4(buf, base, g, receive=True):
        for q in range(4):
            o = (i, xn, yn, dn)[q]
            so = o + 1 - 2 * core
            if receive:
                got(block(buf, base, so), pg_recv.at[g, 4 + q], pg_send.at[g, 4 + q])
            sent(block(buf, base, o), pg_send.at[g, 4 + q], pg_recv.at[g, 4 + q])
        sent(block(buf, base, i), pg_send.at[g, 0], pg_recv.at[g, 0])
        sent(block(buf, base, i), pg_send.at[g, 1], pg_recv.at[g, 1])
        sent(lane_a(buf, base, yn), pg_send.at[g, 2], pg_recv.at[g, 2])
        sent(lane_b(buf, base, xn), pg_send.at[g, 3], pg_recv.at[g, 3])

    low = 1 - j // 2
    edge = low * j + (1 - low) * (nf - 1 - j)

    def shard_of(g):
        place = g + (g + nf - edge) // nf
        return low * place + (1 - low) * (nf - 1 - place)

    def basis_in(g):
        s = shard_of(g)
        got(z_piece(s), z_recv.at[s], z_send.at[0])

        @pl.when((s < j) & (j < nf - 1))
        def _():
            remote(z_piece(s), z_piece(s), z_fwd.at[g], z_recv.at[s], i, j + 1).start()

        @pl.when((s > j) & (j > 0))
        def _():
            remote(z_piece(s), z_piece(s), z_fwd.at[g], z_recv.at[s], i, j - 1).start()

        stage1(rows, s * ndp, g)

    def basis_sent(g):
        s = shard_of(g)

        @pl.when(((s < j) & (j < nf - 1)) | ((s > j) & (j > 0)))
        def _():
            sent(z_piece(s), z_fwd.at[g], z_recv.at[s])

    basis_in(0)

    total = part[j]
    for d in (1, 2, 3):
        z = (j + d) % nf
        got(part_recv.at[z], rs_recv.at[z], rs_send.at[z])
        total = total + part_recv[z].astype(f32)
    proj[j] = total.astype(bf16)
    for d in (1, 2, 3):
        z = (j + d) % nf
        remote(proj.at[j], proj.at[j], ag_send.at[z], ag_recv.at[j], i, z).start()

    stage2(rows, shard_of(0) * ndp, 0)
    basis_in(1)
    stage3(rows, shard_of(0) * ndp, 0)
    stage2(rows, shard_of(1) * ndp, 1)

    for d in (1, 2, 3):
        z = (j + d) % nf
        got(proj.at[z], ag_recv.at[z], ag_send.at[z])

    loads[2].wait()
    projected = proj[...].reshape(tokens, rank)

    def term(k):
        cols = pl.ds(pl.multiple_of(k * own_rows, own_rows), own_rows)
        return lax.dot_general(
            og[:, cols], projected, (((0,), (0,)), ((), ())), preferred_element_type=f32
        ) / total_tokens

    for q in range(4):
        grad[4 + q] = term(2 * q + 1 - core)
        remote(grad.at[4 + q], grad_core.at[q], core_send.at[q], core_recv.at[q], sib, j).start()
    basis_in(2)
    for q in range(4):
        grad[q] = term(2 * q + core)
    for q in range(4):
        got(grad_core.at[q], core_recv.at[q], core_send.at[q])
        grad[q] = grad[q] + grad_core[q]

    for n, far in enumerate((1, 0)):
        yy = far * (1 - y) + (1 - far) * y
        sa1[n] = grad[2 * yy + 1 - x, :, 0:half].astype(bf16)
        remote(sa1.at[n], ra1.at[n], h1_send.at[n], h1_recv.at[n], xn, j).start()
        xx = far * (1 - x) + (1 - far) * x
        sb1[n] = grad[2 * (1 - y) + xx, :, half:rank].astype(bf16)
        remote(sb1.at[n], rb1.at[n], h1_send.at[2 + n], h1_recv.at[2 + n], yn, j).start()
    stage3(rows, shard_of(1) * ndp, 1)
    got(ra1.at[0], h1_recv.at[0], h1_send.at[0])
    sa2[...] = grad[2 * (1 - y) + x, :, 0:half] + ra1[0].astype(f32)
    remote(sa2, ra2, h2_send.at[0], h2_recv.at[0], yn, j).start()
    got(rb1.at[0], h1_recv.at[2], h1_send.at[2])
    sb2[...] = grad[2 * y + 1 - x, :, half:rank] + rb1[0].astype(f32)
    remote(sb2, rb2, h2_send.at[1], h2_recv.at[1], xn, j).start()
    got(ra1.at[1], h1_recv.at[1], h1_send.at[1])
    got(rb1.at[1], h1_recv.at[3], h1_send.at[3])

    stage2(rows, shard_of(2) * ndp, 2)
    mine = 2 * y + x
    loads[3].wait()
    loads[4].wait()
    got(ra2, h2_recv.at[0], h2_send.at[0])
    nf_a, ns_a, up_a = adam(
        first[:, 0:half], second[:, 0:half], grad[mine, :, 0:half] + ra1[1].astype(f32) + ra2[...]
    )
    first[:, 0:half] = nf_a
    second[:, 0:half] = ns_a
    updates[i, :, 0:half] = up_a
    got(rb2, h2_recv.at[1], h2_send.at[1])
    nf_b, ns_b, up_b = adam(
        first[:, half:rank], second[:, half:rank], grad[mine, :, half:rank] + rb1[1].astype(f32) + rb2[...]
    )
    first[:, half:rank] = nf_b
    second[:, half:rank] = ns_b
    updates[i, :, half:rank] = up_b
    stage1(updates, 0, 3)

    store_first = pltpu.make_async_copy(first, first_out, store_sem.at[4])
    store_second = pltpu.make_async_copy(second, second_out, store_sem.at[5])
    store_first.start()
    store_second.start()

    stage3(rows, shard_of(2) * ndp, 2)
    for g in range(3):
        stage4(rows, shard_of(g) * ndp, g)
        basis_sent(g)
    loads[5].wait()

    chunk = 4
    pair_rows = 2 * own_rows
    wide = chunk * own_rows

    def decode(n, o):
        pair = o // 2
        got(block(updates, 0, o + 1 - 2 * core), pg_recv.at[3, 4 + n], pg_send.at[3, 4 + n])
        left = updates[pl.ds(2 * pair, 2)].reshape(pair_rows, rank)
        at = pl.ds(pl.multiple_of(pair * pair_rows, pair_rows), pair_rows)

        def body(c, carry):
            cols = pl.ds(pl.multiple_of(c * wide, wide), wide)
            right = rows[pl.ds(c * chunk, chunk)].reshape(wide, rank)
            decoded = times_basis(left, right)
            weight[at, cols] = (weight[at, cols].astype(f32) - step_rate * decoded).astype(bf16)
            return carry

        lax.fori_loop(0, nf * ndp // chunk, body, 0)
        pltpu.make_async_copy(weight.at[at], weight_out.at[at], store_sem.at[n]).start()

    decode(0, i)
    stage2(updates, 0, 3)
    decode(1, xn)
    stage3(updates, 0, 3)
    decode(2, yn)
    decode(3, dn)
    stage4(updates, 0, 3, False)

    @pl.when(j < nf - 1)
    def _():
        sent(basis_in_ref.at[i], z_send.at[0], z_recv.at[j])

    @pl.when(j > 0)
    def _():
        sent(basis_in_ref.at[i], z_send.at[1], z_recv.at[j])

    for d in (1, 2, 3):
        z = (j + d) % nf
        sent(part_send.at[z], rs_send.at[z], rs_recv.at[z])
        sent(proj.at[j], ag_send.at[z], ag_recv.at[z])
    for q in range(4):
        sent(grad.at[4 + q], core_send.at[q], core_recv.at[q])
    for n in range(2):
        sent(sa1.at[n], h1_send.at[n], h1_recv.at[n])
        sent(sb1.at[n], h1_send.at[2 + n], h1_recv.at[2 + n])
    sent(sa2, h2_send.at[0], h2_recv.at[0])
    sent(sb2, h2_send.at[1], h2_recv.at[1])
    store_first.wait()
    store_second.wait()
    for n, o in enumerate((i, xn, yn, dn)):
        at = pl.ds(pl.multiple_of(o // 2 * pair_rows, pair_rows), pair_rows)
        pltpu.make_async_copy(weight.at[at], weight_out.at[at], store_sem.at[n]).wait()


def local_fused(activations, output_grads, basis, weight, first_moment, second_moment):
    tokens, _ = activations.shape
    shard_rows, rank = basis.shape
    own_rows = first_moment.shape[0]
    ndp, nf = lax.axis_size("dp"), lax.axis_size("fsdp")
    half = rank // 2
    anywhere = pl.BlockSpec(memory_space=pl.ANY)
    dma = pltpu.SemaphoreType.DMA
    return pl.pallas_call(
        fused_kernel,
        out_shape=(
            jax.ShapeDtypeStruct(weight.shape, bf16),
            jax.ShapeDtypeStruct((own_rows, rank), f32),
            jax.ShapeDtypeStruct((own_rows, rank), f32),
        ),
        in_specs=[anywhere] * 6,
        out_specs=(anywhere,) * 3,
        scratch_shapes=[
            pltpu.VMEM(activations.shape, bf16),
            pltpu.VMEM(output_grads.shape, bf16),
            pltpu.VMEM((nf * ndp, own_rows, rank), bf16),
            pltpu.VMEM(weight.shape, bf16),
            pltpu.VMEM((own_rows, rank), f32),
            pltpu.VMEM((own_rows, rank), f32),
            pltpu.VMEM((ndp, own_rows, rank), bf16),
            pltpu.VMEM((nf, tokens // nf, rank), f32),
            pltpu.VMEM((nf, tokens // nf, rank), bf16),
            pltpu.VMEM((nf, tokens // nf, rank), bf16),
            pltpu.VMEM((nf, tokens // nf, rank), bf16),
            pltpu.VMEM((ndp, own_rows, rank), f32),
            pltpu.VMEM((ndp // 2, own_rows, rank), f32),
            pltpu.VMEM((2, own_rows, half), bf16),
            pltpu.VMEM((2, own_rows, half), bf16),
            pltpu.VMEM((2, own_rows, half), bf16),
            pltpu.VMEM((2, own_rows, half), bf16),
            pltpu.VMEM((own_rows, half), f32),
            pltpu.VMEM((own_rows, half), f32),
            pltpu.VMEM((own_rows, half), f32),
            pltpu.VMEM((own_rows, half), f32),
            dma((6,)), dma((6,)), dma((2,)), dma((3,)), dma((nf,)), dma((nf,)), dma((nf,)), dma((nf,)), dma((nf,)),
            dma((4,)), dma((4,)), dma((4,)), dma((4,)), dma((2,)), dma((2,)), dma((4, 8)), dma((4, 8)),
        ],
        compiler_params=pltpu.CompilerParams(
            collective_id=0, has_side_effects=True, vmem_limit_bytes=63 * 1024 * 1024
        ),
        cost_estimate=pl.CostEstimate(
            flops=2 * shard_rows * rank * (2 * tokens + nf * shard_rows), bytes_accessed=24 * 1024 * 1024, transcendentals=0
        ),
    )(
        activations, output_grads, basis.reshape(ndp, own_rows, rank), weight,
        first_moment, second_moment,
    )


def local(activations, output_grads, basis, weight, first_moment, second_moment):
    partial_product = jnp.dot(activations, basis, preferred_element_type=f32)
    projected = lax.psum(partial_product, "fsdp").astype(bf16)
    total_tokens = projected.shape[0] * lax.axis_size("dp")
    local_term = (
        lax.dot_general(
            output_grads, projected, (((0,), (0,)), ((), ())), preferred_element_type=f32
        )
        / total_tokens
    )
    low_grad = lax.psum_scatter(local_term, "dp", scatter_dimension=0, tiled=True)
    new_first, new_second, update = adam(first_moment, second_moment, low_grad)
    all_updates = lax.all_gather(update, "dp", axis=0, tiled=True)
    decoded = times_basis(all_updates, lax.all_gather(basis, "fsdp", axis=0, tiled=True))
    new_weight = (weight.astype(f32) - step_rate * decoded).astype(bf16)
    return (new_weight, new_first, new_second)


def solution(mesh):
    fused = mesh.shape["dp"] == 8 and mesh.shape["fsdp"] == 4
    return jax.shard_map(
        local_fused if fused else local,
        mesh=mesh,
        in_specs=(
            P("dp", "fsdp"),
            P("dp", "fsdp"),
            P("fsdp", None),
            P("fsdp", None),
            P(("fsdp", "dp"), None),
            P(("fsdp", "dp"), None),
        ),
        out_specs=(P("fsdp", None), P(("fsdp", "dp"), None), P(("fsdp", "dp"), None)),
        check_vma=False,
    )
```

```python
import functools

import jax
import jax.numpy as jnp
from jax import lax
from jax.experimental import pallas as pl
from jax.experimental.pallas import tpu as pltpu
from jax.sharding import PartitionSpec as P

first_decay = 0.9
second_decay = 0.999
first_fix = 1.0 - 0.9**10
second_fix = 1.0 - 0.999**10
step_rate = 0.01
tiny_eps = 1e-08
MESH = pl.DeviceIdType.MESH
f32 = jnp.float32
bf16 = jnp.bfloat16


def times_basis(update, rows):
    return lax.dot_general(update, rows, (((1,), (1,)), ((), ())), preferred_element_type=f32)


def adam(first, second, low_grad):
    new_first = first_decay * first + (1.0 - first_decay) * low_grad
    new_second = second_decay * second + (1.0 - second_decay) * low_grad * low_grad
    update = (new_first / first_fix / (jnp.sqrt(new_second / second_fix) + tiny_eps)).astype(bf16)
    return new_first, new_second, update


def fused_kernel(
    act_in, og_in, basis_in_ref, weight_in, first_in, second_in,
    weight_out, first_out, second_out,
    act, og, rows, weight, first, second, updates,
    part, part_send, part_recv, proj,
    grad, grad_core, sa1, sb1, ra1, rb1, sa2, sb2, ra2, rb2,
    load_sem, store_sem, z_send, z_fwd, z_recv, rs_send, rs_recv, ag_send, ag_recv,
    core_send, core_recv, h1_send, h1_recv, h2_send, h2_recv, pg_send, pg_recv,
):
    i = lax.axis_index("dp")
    j = lax.axis_index("fsdp")
    ndp, nf = 8, 4
    core, x, y = i % 2, (i // 2) % 2, i // 4
    sib = i + 1 - 2 * core
    xn = i + 2 * (1 - 2 * x)
    yn = i + 4 * (1 - 2 * y)
    dn = xn + 4 * (1 - 2 * y)
    tokens, rank = act.shape[0], first.shape[1]
    own_rows = first.shape[0]
    tb = tokens // nf
    half = rank // 2
    total_tokens = tokens * ndp

    loads = [
        pltpu.make_async_copy(src, dst, load_sem.at[n])
        for n, (src, dst) in enumerate((
            (act_in, act),
            (basis_in_ref, rows.at[pl.ds(j * ndp, ndp)]),
            (og_in, og),
            (first_in, first),
            (second_in, second),
            (weight_in, weight),
        ))
    ]
    for load in loads:
        load.start()

    def remote(src, dst, ssem, rsem, dp, z):
        return pltpu.make_async_remote_copy(
            src_ref=src, dst_ref=dst, send_sem=ssem, recv_sem=rsem,
            device_id=(dp, z), device_id_type=MESH,
        )

    def got(dst, rsem, ssem):
        remote(dst, dst, ssem, rsem, sib, j).wait_recv()

    def sent(src, ssem, rsem):
        remote(src, src, ssem, rsem, sib, j).wait_send()

    barrier = pltpu.get_barrier_semaphore()
    for dp in (sib, xn, yn):
        pl.semaphore_signal(barrier, inc=1, device_id=(dp, j), device_id_type=MESH)
    for d in range(1, nf):
        pl.semaphore_signal(barrier, inc=1, device_id=(i, (j + d) % nf), device_id_type=MESH)
    pl.semaphore_wait(barrier, 3 + nf - 1)

    def z_piece(shard):
        return rows.at[shard * ndp + i]

    @pl.when(j < nf - 1)
    def _():
        remote(basis_in_ref.at[i], z_piece(j), z_send.at[0], z_recv.at[j], i, j + 1).start()

    @pl.when(j > 0)
    def _():
        remote(basis_in_ref.at[i], z_piece(j), z_send.at[1], z_recv.at[j], i, j - 1).start()

    loads[0].wait()
    loads[1].wait()
    a = act[...]
    acc = None
    for k in range(ndp):
        term = jnp.dot(a[:, k * own_rows : (k + 1) * own_rows], rows[j * ndp + k], preferred_element_type=f32)
        acc = term if acc is None else acc + term
    part[...] = acc.reshape(nf, tb, rank)
    part_send[...] = acc.reshape(nf, tb, rank).astype(bf16)
    for d in (1, 2, 3):
        z = (j + d) % nf
        remote(part_send.at[z], part_recv.at[j], rs_send.at[z], rs_recv.at[j], i, z).start()

    def block(buf, base, k):
        return buf.at[base + k]

    def lane_a(buf, base, k):
        return buf.at[base + k, :, pl.ds(0, half)]

    def lane_b(buf, base, k):
        return buf.at[base + k, :, pl.ds(half, half)]

    def stage1(buf, base, g):
        mine = block(buf, base, i)
        remote(mine, mine, pg_send.at[g, 0], pg_recv.at[g, 0], xn, j).start()
        remote(mine, mine, pg_send.at[g, 1], pg_recv.at[g, 1], yn, j).start()
        remote(mine, mine, pg_send.at[g, 4], pg_recv.at[g, 4], sib, j).start()

    def stage2(buf, base, g):
        bx, by = block(buf, base, xn), block(buf, base, yn)
        got(bx, pg_recv.at[g, 0], pg_send.at[g, 0])
        lb = lane_b(buf, base, xn)
        remote(lb, lb, pg_send.at[g, 3], pg_recv.at[g, 3], yn, j).start()
        remote(bx, bx, pg_send.at[g, 5], pg_recv.at[g, 5], sib, j).start()
        got(by, pg_recv.at[g, 1], pg_send.at[g, 1])
        la = lane_a(buf, base, yn)
        remote(la, la, pg_send.at[g, 2], pg_recv.at[g, 2], xn, j).start()
        remote(by, by, pg_send.at[g, 6], pg_recv.at[g, 6], sib, j).start()

    def stage3(buf, base, g):
        got(lane_a(buf, base, dn), pg_recv.at[g, 2], pg_send.at[g, 2])
        got(lane_b(buf, base, dn), pg_recv.at[g, 3], pg_send.at[g, 3])
        bd = block(buf, base, dn)
        remote(bd, bd, pg_send.at[g, 7], pg_recv.at[g, 7], sib, j).start()

    def stage4(buf, base, g, receive=True):
        for q in range(4):
            o = (i, xn, yn, dn)[q]
            so = o + 1 - 2 * core
            if receive:
                got(block(buf, base, so), pg_recv.at[g, 4 + q], pg_send.at[g, 4 + q])
            sent(block(buf, base, o), pg_send.at[g, 4 + q], pg_recv.at[g, 4 + q])
        sent(block(buf, base, i), pg_send.at[g, 0], pg_recv.at[g, 0])
        sent(block(buf, base, i), pg_send.at[g, 1], pg_recv.at[g, 1])
        sent(lane_a(buf, base, yn), pg_send.at[g, 2], pg_recv.at[g, 2])
        sent(lane_b(buf, base, xn), pg_send.at[g, 3], pg_recv.at[g, 3])

    low = 1 - j // 2
    edge = low * j + (1 - low) * (nf - 1 - j)

    def shard_of(g):
        place = g + (g + nf - edge) // nf
        return low * place + (1 - low) * (nf - 1 - place)

    def basis_in(g):
        s = shard_of(g)
        got(z_piece(s), z_recv.at[s], z_send.at[0])

        @pl.when((s < j) & (j < nf - 1))
        def _():
            remote(z_piece(s), z_piece(s), z_fwd.at[g], z_recv.at[s], i, j + 1).start()

        @pl.when((s > j) & (j > 0))
        def _():
            remote(z_piece(s), z_piece(s), z_fwd.at[g], z_recv.at[s], i, j - 1).start()

        stage1(rows, s * ndp, g)

    def basis_sent(g):
        s = shard_of(g)

        @pl.when(((s < j) & (j < nf - 1)) | ((s > j) & (j > 0)))
        def _():
            sent(z_piece(s), z_fwd.at[g], z_recv.at[s])

    basis_in(0)
    basis_in(1)

    total = part[j]
    for d in (1, 2, 3):
        z = (j + d) % nf
        got(part_recv.at[z], rs_recv.at[z], rs_send.at[z])
        total = total + part_recv[z].astype(f32)
    proj[j] = total.astype(bf16)
    for d in (1, 2, 3):
        z = (j + d) % nf
        remote(proj.at[j], proj.at[j], ag_send.at[z], ag_recv.at[j], i, z).start()

    stage2(rows, shard_of(0) * ndp, 0)
    basis_in(2)
    stage3(rows, shard_of(0) * ndp, 0)
    stage2(rows, shard_of(1) * ndp, 1)

    for d in (1, 2, 3):
        z = (j + d) % nf
        got(proj.at[z], ag_recv.at[z], ag_send.at[z])

    loads[2].wait()
    projected = proj[...].reshape(tokens, rank)

    def term(k):
        cols = pl.ds(pl.multiple_of(k * own_rows, own_rows), own_rows)
        return lax.dot_general(
            og[:, cols], projected, (((0,), (0,)), ((), ())), preferred_element_type=f32
        ) / total_tokens

    mine = 2 * y + x
    order = (3 - mine, 2 * y + 1 - x, 2 * (1 - y) + x, mine)
    for q in range(4):
        grad[4 + q] = term(2 * order[q] + 1 - core)
        remote(grad.at[4 + q], grad_core.at[q], core_send.at[q], core_recv.at[q], sib, j).start()
    for q in range(4):
        grad[q] = term(2 * order[q] + core)

    def pair_sum(q):
        got(grad_core.at[q], core_recv.at[q], core_send.at[q])
        grad[q] = grad[q] + grad_core[q]

    def hop1(n, qa, qb):
        if qa is not None:
            sa1[n] = grad[qa, :, 0:half].astype(bf16)
            remote(sa1.at[n], ra1.at[n], h1_send.at[n], h1_recv.at[n], xn, j).start()
        if qb is not None:
            sb1[n] = grad[qb, :, half:rank].astype(bf16)
            remote(sb1.at[n], rb1.at[n], h1_send.at[2 + n], h1_recv.at[2 + n], yn, j).start()

    pair_sum(0)
    hop1(0, 0, 0)
    pair_sum(1)
    hop1(1, 1, None)
    pair_sum(2)
    hop1(1, None, 2)
    pair_sum(3)
    stage3(rows, shard_of(1) * ndp, 1)
    stage2(rows, shard_of(2) * ndp, 2)
    got(ra1.at[0], h1_recv.at[0], h1_send.at[0])
    sa2[...] = grad[2, :, 0:half] + ra1[0].astype(f32)
    remote(sa2, ra2, h2_send.at[0], h2_recv.at[0], yn, j).start()
    got(rb1.at[0], h1_recv.at[2], h1_send.at[2])
    sb2[...] = grad[1, :, half:rank] + rb1[0].astype(f32)
    remote(sb2, rb2, h2_send.at[1], h2_recv.at[1], xn, j).start()
    got(ra1.at[1], h1_recv.at[1], h1_send.at[1])
    got(rb1.at[1], h1_recv.at[3], h1_send.at[3])

    stage3(rows, shard_of(2) * ndp, 2)
    loads[3].wait()
    loads[4].wait()
    got(ra2, h2_recv.at[0], h2_send.at[0])
    nf_a, ns_a, up_a = adam(
        first[:, 0:half], second[:, 0:half], grad[3, :, 0:half] + ra1[1].astype(f32) + ra2[...]
    )
    first[:, 0:half] = nf_a
    second[:, 0:half] = ns_a
    updates[i, :, 0:half] = up_a
    got(rb2, h2_recv.at[1], h2_send.at[1])
    nf_b, ns_b, up_b = adam(
        first[:, half:rank], second[:, half:rank], grad[3, :, half:rank] + rb1[1].astype(f32) + rb2[...]
    )
    first[:, half:rank] = nf_b
    second[:, half:rank] = ns_b
    updates[i, :, half:rank] = up_b
    stage1(updates, 0, 3)

    store_first = pltpu.make_async_copy(first, first_out, store_sem.at[4])
    store_second = pltpu.make_async_copy(second, second_out, store_sem.at[5])
    store_first.start()
    store_second.start()

    for g in range(3):
        stage4(rows, shard_of(g) * ndp, g)
        basis_sent(g)
    loads[5].wait()

    chunk = 4
    pair_rows = 2 * own_rows
    wide = chunk * own_rows

    def decode(n, o):
        pair = o // 2
        got(block(updates, 0, o + 1 - 2 * core), pg_recv.at[3, 4 + n], pg_send.at[3, 4 + n])
        left = updates[pl.ds(2 * pair, 2)].reshape(pair_rows, rank)
        at = pl.ds(pl.multiple_of(pair * pair_rows, pair_rows), pair_rows)

        def body(c, carry):
            cols = pl.ds(pl.multiple_of(c * wide, wide), wide)
            right = rows[pl.ds(c * chunk, chunk)].reshape(wide, rank)
            decoded = times_basis(left, right)
            weight[at, cols] = (weight[at, cols].astype(f32) - step_rate * decoded).astype(bf16)
            return carry

        lax.fori_loop(0, nf * ndp // chunk, body, 0)
        pltpu.make_async_copy(weight.at[at], weight_out.at[at], store_sem.at[n]).start()

    decode(0, i)
    stage2(updates, 0, 3)
    decode(1, xn)
    stage3(updates, 0, 3)
    decode(2, yn)
    decode(3, dn)
    stage4(updates, 0, 3, False)

    @pl.when(j < nf - 1)
    def _():
        sent(basis_in_ref.at[i], z_send.at[0], z_recv.at[j])

    @pl.when(j > 0)
    def _():
        sent(basis_in_ref.at[i], z_send.at[1], z_recv.at[j])

    for d in (1, 2, 3):
        z = (j + d) % nf
        sent(part_send.at[z], rs_send.at[z], rs_recv.at[z])
        sent(proj.at[j], ag_send.at[z], ag_recv.at[z])
    for q in range(4):
        sent(grad.at[4 + q], core_send.at[q], core_recv.at[q])
    for n in range(2):
        sent(sa1.at[n], h1_send.at[n], h1_recv.at[n])
        sent(sb1.at[n], h1_send.at[2 + n], h1_recv.at[2 + n])
    sent(sa2, h2_send.at[0], h2_recv.at[0])
    sent(sb2, h2_send.at[1], h2_recv.at[1])
    store_first.wait()
    store_second.wait()
    for n, o in enumerate((i, xn, yn, dn)):
        at = pl.ds(pl.multiple_of(o // 2 * pair_rows, pair_rows), pair_rows)
        pltpu.make_async_copy(weight.at[at], weight_out.at[at], store_sem.at[n]).wait()


def store_kernel(*refs):
    n = len(refs) // 2
    sources, targets, sem = refs[:n], refs[n : 2 * n], refs[2 * n]
    copies = []
    for source, target in zip(sources, targets):
        pieces = 8 if source.dtype == bf16 else 1
        size = source.shape[0] // pieces
        for k in range(pieces):
            at = pl.ds(k * size, size)
            copies.append(pltpu.make_async_copy(source.at[at], target.at[at], sem.at[len(copies)]))
    for copy in copies:
        copy.start()
    for copy in copies:
        copy.wait()


def local_fused(activations, output_grads, basis, weight, first_moment, second_moment):
    tokens, _ = activations.shape
    shard_rows, rank = basis.shape
    own_rows = first_moment.shape[0]
    ndp, nf = lax.axis_size("dp"), lax.axis_size("fsdp")
    half = rank // 2
    anywhere = pl.BlockSpec(memory_space=pl.ANY)
    dma = pltpu.SemaphoreType.DMA
    results = pl.pallas_call(
        fused_kernel,
        out_shape=(
            jax.ShapeDtypeStruct(weight.shape, bf16),
            jax.ShapeDtypeStruct((own_rows, rank), f32),
            jax.ShapeDtypeStruct((own_rows, rank), f32),
        ),
        in_specs=[anywhere] * 6,
        out_specs=(anywhere,) * 3,
        scratch_shapes=[
            pltpu.VMEM(activations.shape, bf16),
            pltpu.VMEM(output_grads.shape, bf16),
            pltpu.VMEM((nf * ndp, own_rows, rank), bf16),
            pltpu.VMEM(weight.shape, bf16),
            pltpu.VMEM((own_rows, rank), f32),
            pltpu.VMEM((own_rows, rank), f32),
            pltpu.VMEM((ndp, own_rows, rank), bf16),
            pltpu.VMEM((nf, tokens // nf, rank), f32),
            pltpu.VMEM((nf, tokens // nf, rank), bf16),
            pltpu.VMEM((nf, tokens // nf, rank), bf16),
            pltpu.VMEM((nf, tokens // nf, rank), bf16),
            pltpu.VMEM((ndp, own_rows, rank), f32),
            pltpu.VMEM((ndp // 2, own_rows, rank), f32),
            pltpu.VMEM((2, own_rows, half), bf16),
            pltpu.VMEM((2, own_rows, half), bf16),
            pltpu.VMEM((2, own_rows, half), bf16),
            pltpu.VMEM((2, own_rows, half), bf16),
            pltpu.VMEM((own_rows, half), f32),
            pltpu.VMEM((own_rows, half), f32),
            pltpu.VMEM((own_rows, half), f32),
            pltpu.VMEM((own_rows, half), f32),
            dma((6,)), dma((6,)), dma((2,)), dma((3,)), dma((nf,)), dma((nf,)), dma((nf,)), dma((nf,)), dma((nf,)),
            dma((4,)), dma((4,)), dma((4,)), dma((4,)), dma((2,)), dma((2,)), dma((4, 8)), dma((4, 8)),
        ],
        compiler_params=pltpu.CompilerParams(
            collective_id=0, has_side_effects=True, vmem_limit_bytes=63 * 1024 * 1024
        ),
        cost_estimate=pl.CostEstimate(
            flops=2 * shard_rows * rank * (2 * tokens + nf * shard_rows), bytes_accessed=24 * 1024 * 1024, transcendentals=0
        ),
    )(
        activations, output_grads, basis.reshape(ndp, own_rows, rank), weight,
        first_moment, second_moment,
    )
    return pl.pallas_call(
        store_kernel,
        out_shape=[jax.ShapeDtypeStruct(r.shape, r.dtype) for r in results],
        in_specs=[anywhere] * 3,
        out_specs=[anywhere] * 3,
        scratch_shapes=[dma((10,))],
        compiler_params=pltpu.CompilerParams(vmem_limit_bytes=63 * 1024 * 1024),
    )(*results)


def local(activations, output_grads, basis, weight, first_moment, second_moment):
    partial_product = jnp.dot(activations, basis, preferred_element_type=f32)
    projected = lax.psum(partial_product, "fsdp").astype(bf16)
    total_tokens = projected.shape[0] * lax.axis_size("dp")
    local_term = (
        lax.dot_general(
            output_grads, projected, (((0,), (0,)), ((), ())), preferred_element_type=f32
        )
        / total_tokens
    )
    low_grad = lax.psum_scatter(local_term, "dp", scatter_dimension=0, tiled=True)
    new_first, new_second, update = adam(first_moment, second_moment, low_grad)
    all_updates = lax.all_gather(update, "dp", axis=0, tiled=True)
    decoded = times_basis(all_updates, lax.all_gather(basis, "fsdp", axis=0, tiled=True))
    new_weight = (weight.astype(f32) - step_rate * decoded).astype(bf16)
    return (new_weight, new_first, new_second)


def solution(mesh):
    fused = mesh.shape["dp"] == 8 and mesh.shape["fsdp"] == 4
    return jax.shard_map(
        local_fused if fused else local,
        mesh=mesh,
        in_specs=(
            P("dp", "fsdp"),
            P("dp", "fsdp"),
            P("fsdp", None),
            P("fsdp", None),
            P(("fsdp", "dp"), None),
            P(("fsdp", "dp"), None),
        ),
        out_specs=(P("fsdp", None), P(("fsdp", "dp"), None), P(("fsdp", "dp"), None)),
        check_vma=False,
    )
```

```python
import functools

import jax
import jax.numpy as jnp
from jax import lax
from jax.experimental import pallas as pl
from jax.experimental.pallas import tpu as pltpu
from jax.sharding import PartitionSpec as P

first_decay = 0.9
second_decay = 0.999
first_fix = 1.0 - 0.9**10
second_fix = 1.0 - 0.999**10
step_rate = 0.01
tiny_eps = 1e-08
MESH = pl.DeviceIdType.MESH
f32 = jnp.float32
bf16 = jnp.bfloat16


def times_basis(update, rows):
    return lax.dot_general(update, rows, (((1,), (1,)), ((), ())), preferred_element_type=f32)


def adam(first, second, low_grad):
    new_first = first_decay * first + (1.0 - first_decay) * low_grad
    new_second = second_decay * second + (1.0 - second_decay) * low_grad * low_grad
    update = (new_first / first_fix / (jnp.sqrt(new_second / second_fix) + tiny_eps)).astype(bf16)
    return new_first, new_second, update


def fused_kernel(
    act_in, og_in, basis_in_ref, weight_in, first_in, second_in,
    weight_out, first_out, second_out,
    act, og, rows, weight, first, second, updates,
    part, part_send, part_recv, proj,
    grad, grad_core, sa1, sb1, ra1, rb1, sa2, sb2, ra2, rb2,
    load_sem, store_sem, z_send, z_fwd, z_recv, rs_send, rs_recv, ag_send, ag_recv,
    core_send, core_recv, h1_send, h1_recv, h2_send, h2_recv, pg_send, pg_recv,
):
    i = lax.axis_index("dp")
    j = lax.axis_index("fsdp")
    ndp, nf = 8, 4
    core, x, y = i % 2, (i // 2) % 2, i // 4
    sib = i + 1 - 2 * core
    xn = i + 2 * (1 - 2 * x)
    yn = i + 4 * (1 - 2 * y)
    dn = xn + 4 * (1 - 2 * y)
    tokens, rank = act.shape[0], first.shape[1]
    own_rows = first.shape[0]
    tb = tokens // nf
    half = rank // 2
    total_tokens = tokens * ndp

    loads = [
        pltpu.make_async_copy(src, dst, load_sem.at[n])
        for n, (src, dst) in enumerate((
            (act_in, act),
            (basis_in_ref, rows.at[pl.ds(j * ndp, ndp)]),
            (og_in, og),
            (first_in, first),
            (second_in, second),
            (weight_in, weight),
        ))
    ]
    for load in loads:
        load.start()

    def remote(src, dst, ssem, rsem, dp, z):
        return pltpu.make_async_remote_copy(
            src_ref=src, dst_ref=dst, send_sem=ssem, recv_sem=rsem,
            device_id=(dp, z), device_id_type=MESH,
        )

    def got(dst, rsem, ssem):
        remote(dst, dst, ssem, rsem, sib, j).wait_recv()

    def sent(src, ssem, rsem):
        remote(src, src, ssem, rsem, sib, j).wait_send()

    barrier = pltpu.get_barrier_semaphore()
    for dp in (sib, xn, yn):
        pl.semaphore_signal(barrier, inc=1, device_id=(dp, j), device_id_type=MESH)
    for d in range(1, nf):
        pl.semaphore_signal(barrier, inc=1, device_id=(i, (j + d) % nf), device_id_type=MESH)
    pl.semaphore_wait(barrier, 3 + nf - 1)

    def z_piece(shard):
        return rows.at[shard * ndp + i]

    @pl.when(j < nf - 1)
    def _():
        remote(basis_in_ref.at[i], z_piece(j), z_send.at[0], z_recv.at[j], i, j + 1).start()

    @pl.when(j > 0)
    def _():
        remote(basis_in_ref.at[i], z_piece(j), z_send.at[1], z_recv.at[j], i, j - 1).start()

    loads[0].wait()
    loads[1].wait()
    acc = jnp.dot(
        act[...],
        rows[pl.ds(j * ndp, ndp)].reshape(ndp * own_rows, rank),
        preferred_element_type=f32,
    )
    part[...] = acc.reshape(nf, tb, rank)
    part_send[...] = acc.reshape(nf, tb, rank).astype(bf16)
    for d in (1, 2, 3):
        z = (j + d) % nf
        remote(part_send.at[z], part_recv.at[j], rs_send.at[z], rs_recv.at[j], i, z).start()

    def block(buf, base, k):
        return buf.at[base + k]

    def lane_a(buf, base, k):
        return buf.at[base + k, :, pl.ds(0, half)]

    def lane_b(buf, base, k):
        return buf.at[base + k, :, pl.ds(half, half)]

    def stage1(buf, base, g):
        mine = block(buf, base, i)
        remote(mine, mine, pg_send.at[g, 0], pg_recv.at[g, 0], xn, j).start()
        remote(mine, mine, pg_send.at[g, 1], pg_recv.at[g, 1], yn, j).start()
        remote(mine, mine, pg_send.at[g, 4], pg_recv.at[g, 4], sib, j).start()

    def stage2(buf, base, g):
        bx, by = block(buf, base, xn), block(buf, base, yn)
        got(bx, pg_recv.at[g, 0], pg_send.at[g, 0])
        lb = lane_b(buf, base, xn)
        remote(lb, lb, pg_send.at[g, 3], pg_recv.at[g, 3], yn, j).start()
        remote(bx, bx, pg_send.at[g, 5], pg_recv.at[g, 5], sib, j).start()
        got(by, pg_recv.at[g, 1], pg_send.at[g, 1])
        la = lane_a(buf, base, yn)
        remote(la, la, pg_send.at[g, 2], pg_recv.at[g, 2], xn, j).start()
        remote(by, by, pg_send.at[g, 6], pg_recv.at[g, 6], sib, j).start()

    def stage3(buf, base, g):
        got(lane_a(buf, base, dn), pg_recv.at[g, 2], pg_send.at[g, 2])
        got(lane_b(buf, base, dn), pg_recv.at[g, 3], pg_send.at[g, 3])
        bd = block(buf, base, dn)
        remote(bd, bd, pg_send.at[g, 7], pg_recv.at[g, 7], sib, j).start()

    def stage4(buf, base, g, receive=True):
        for q in range(4):
            o = (i, xn, yn, dn)[q]
            so = o + 1 - 2 * core
            if receive:
                got(block(buf, base, so), pg_recv.at[g, 4 + q], pg_send.at[g, 4 + q])
            sent(block(buf, base, o), pg_send.at[g, 4 + q], pg_recv.at[g, 4 + q])
        sent(block(buf, base, i), pg_send.at[g, 0], pg_recv.at[g, 0])
        sent(block(buf, base, i), pg_send.at[g, 1], pg_recv.at[g, 1])
        sent(lane_a(buf, base, yn), pg_send.at[g, 2], pg_recv.at[g, 2])
        sent(lane_b(buf, base, xn), pg_send.at[g, 3], pg_recv.at[g, 3])

    low = 1 - j // 2
    edge = low * j + (1 - low) * (nf - 1 - j)

    def shard_of(g):
        place = g + (g + nf - edge) // nf
        return low * place + (1 - low) * (nf - 1 - place)

    def basis_in(g):
        s = shard_of(g)
        got(z_piece(s), z_recv.at[s], z_send.at[0])

        @pl.when((s < j) & (j < nf - 1))
        def _():
            remote(z_piece(s), z_piece(s), z_fwd.at[g], z_recv.at[s], i, j + 1).start()

        @pl.when((s > j) & (j > 0))
        def _():
            remote(z_piece(s), z_piece(s), z_fwd.at[g], z_recv.at[s], i, j - 1).start()

        stage1(rows, s * ndp, g)

    def basis_sent(g):
        s = shard_of(g)

        @pl.when(((s < j) & (j < nf - 1)) | ((s > j) & (j > 0)))
        def _():
            sent(z_piece(s), z_fwd.at[g], z_recv.at[s])

    basis_in(0)
    basis_in(1)

    total = part[j]
    for d in (1, 2, 3):
        z = (j + d) % nf
        got(part_recv.at[z], rs_recv.at[z], rs_send.at[z])
        total = total + part_recv[z].astype(f32)
    proj[j] = total.astype(bf16)
    for d in (1, 2, 3):
        z = (j + d) % nf
        remote(proj.at[j], proj.at[j], ag_send.at[z], ag_recv.at[j], i, z).start()

    stage2(rows, shard_of(0) * ndp, 0)
    basis_in(2)
    stage3(rows, shard_of(0) * ndp, 0)
    stage2(rows, shard_of(1) * ndp, 1)

    for d in (1, 2, 3):
        z = (j + d) % nf
        got(proj.at[z], ag_recv.at[z], ag_send.at[z])

    loads[2].wait()
    projected = proj[...].reshape(tokens, rank)

    def term(k):
        cols = pl.ds(pl.multiple_of(k * own_rows, own_rows), own_rows)
        return lax.dot_general(
            og[:, cols], projected, (((0,), (0,)), ((), ())), preferred_element_type=f32
        )

    mine = 2 * y + x
    order = (3 - mine, 2 * y + 1 - x, 2 * (1 - y) + x, mine)
    for q in range(4):
        grad[4 + q] = term(2 * order[q] + 1 - core)
        remote(grad.at[4 + q], grad_core.at[q], core_send.at[q], core_recv.at[q], sib, j).start()
    for q in range(4):
        grad[q] = term(2 * order[q] + core)

    def pair_sum(q):
        got(grad_core.at[q], core_recv.at[q], core_send.at[q])
        grad[q] = grad[q] + grad_core[q]

    def hop1(n, qa, qb):
        if qa is not None:
            sa1[n] = grad[qa, :, 0:half].astype(bf16)
            remote(sa1.at[n], ra1.at[n], h1_send.at[n], h1_recv.at[n], xn, j).start()
        if qb is not None:
            sb1[n] = grad[qb, :, half:rank].astype(bf16)
            remote(sb1.at[n], rb1.at[n], h1_send.at[2 + n], h1_recv.at[2 + n], yn, j).start()

    pair_sum(0)
    hop1(0, 0, 0)
    pair_sum(1)
    hop1(1, 1, None)
    pair_sum(2)
    hop1(1, None, 2)
    pair_sum(3)
    stage3(rows, shard_of(1) * ndp, 1)
    stage2(rows, shard_of(2) * ndp, 2)
    got(ra1.at[0], h1_recv.at[0], h1_send.at[0])
    sa2[...] = grad[2, :, 0:half] + ra1[0].astype(f32)
    remote(sa2, ra2, h2_send.at[0], h2_recv.at[0], yn, j).start()
    got(rb1.at[0], h1_recv.at[2], h1_send.at[2])
    sb2[...] = grad[1, :, half:rank] + rb1[0].astype(f32)
    remote(sb2, rb2, h2_send.at[1], h2_recv.at[1], xn, j).start()
    got(ra1.at[1], h1_recv.at[1], h1_send.at[1])
    got(rb1.at[1], h1_recv.at[3], h1_send.at[3])

    stage3(rows, shard_of(2) * ndp, 2)
    loads[3].wait()
    loads[4].wait()
    got(ra2, h2_recv.at[0], h2_send.at[0])
    nf_a, ns_a, up_a = adam(
        first[:, 0:half], second[:, 0:half], (grad[3, :, 0:half] + ra1[1].astype(f32) + ra2[...]) / total_tokens
    )
    first[:, 0:half] = nf_a
    second[:, 0:half] = ns_a
    updates[i, :, 0:half] = up_a
    got(rb2, h2_recv.at[1], h2_send.at[1])
    nf_b, ns_b, up_b = adam(
        first[:, half:rank], second[:, half:rank], (grad[3, :, half:rank] + rb1[1].astype(f32) + rb2[...]) / total_tokens
    )
    first[:, half:rank] = nf_b
    second[:, half:rank] = ns_b
    updates[i, :, half:rank] = up_b
    stage1(updates, 0, 3)

    store_first = pltpu.make_async_copy(first, first_out, store_sem.at[4])
    store_second = pltpu.make_async_copy(second, second_out, store_sem.at[5])
    store_first.start()
    store_second.start()

    for g in range(3):
        stage4(rows, shard_of(g) * ndp, g)
        basis_sent(g)
    loads[5].wait()

    chunk = 4
    pair_rows = 2 * own_rows
    wide = chunk * own_rows

    def decode(n, o):
        pair = o // 2
        got(block(updates, 0, o + 1 - 2 * core), pg_recv.at[3, 4 + n], pg_send.at[3, 4 + n])
        left = updates[pl.ds(2 * pair, 2)].reshape(pair_rows, rank)
        at = pl.ds(pl.multiple_of(pair * pair_rows, pair_rows), pair_rows)

        def body(c, carry):
            cols = pl.ds(pl.multiple_of(c * wide, wide), wide)
            right = rows[pl.ds(c * chunk, chunk)].reshape(wide, rank)
            decoded = times_basis(left, right)
            weight[at, cols] = (weight[at, cols].astype(f32) - step_rate * decoded).astype(bf16)
            return carry

        lax.fori_loop(0, nf * ndp // chunk, body, 0)
        pltpu.make_async_copy(weight.at[at], weight_out.at[at], store_sem.at[n]).start()

    decode(0, i)
    stage2(updates, 0, 3)
    decode(1, xn)
    stage3(updates, 0, 3)
    decode(2, yn)
    decode(3, dn)
    stage4(updates, 0, 3, False)

    @pl.when(j < nf - 1)
    def _():
        sent(basis_in_ref.at[i], z_send.at[0], z_recv.at[j])

    @pl.when(j > 0)
    def _():
        sent(basis_in_ref.at[i], z_send.at[1], z_recv.at[j])

    for d in (1, 2, 3):
        z = (j + d) % nf
        sent(part_send.at[z], rs_send.at[z], rs_recv.at[z])
        sent(proj.at[j], ag_send.at[z], ag_recv.at[z])
    for q in range(4):
        sent(grad.at[4 + q], core_send.at[q], core_recv.at[q])
    for n in range(2):
        sent(sa1.at[n], h1_send.at[n], h1_recv.at[n])
        sent(sb1.at[n], h1_send.at[2 + n], h1_recv.at[2 + n])
    sent(sa2, h2_send.at[0], h2_recv.at[0])
    sent(sb2, h2_send.at[1], h2_recv.at[1])
    store_first.wait()
    store_second.wait()
    for n, o in enumerate((i, xn, yn, dn)):
        at = pl.ds(pl.multiple_of(o // 2 * pair_rows, pair_rows), pair_rows)
        pltpu.make_async_copy(weight.at[at], weight_out.at[at], store_sem.at[n]).wait()


def store_kernel(
    weight, first, second, weight_out, first_out, second_out,
    weight_buf, first_buf, second_buf, in_sem, out_sem,
):
    pieces = 16
    size = weight.shape[0] // pieces
    parts = [
        (weight.at[pl.ds(k * size, size)], weight_buf.at[pl.ds(k * size, size)],
         weight_out.at[pl.ds(k * size, size)])
        for k in range(pieces)
    ] + [(first, first_buf, first_out), (second, second_buf, second_out)]
    ins = [pltpu.make_async_copy(a, b, in_sem.at[n]) for n, (a, b, _) in enumerate(parts)]
    outs = [pltpu.make_async_copy(b, c, out_sem.at[n]) for n, (_, b, c) in enumerate(parts)]
    for copy in ins:
        copy.start()
    for load, store in zip(ins, outs):
        load.wait()
        store.start()
    for copy in outs:
        copy.wait()


def local_fused(activations, output_grads, basis, weight, first_moment, second_moment):
    tokens, _ = activations.shape
    shard_rows, rank = basis.shape
    own_rows = first_moment.shape[0]
    ndp, nf = lax.axis_size("dp"), lax.axis_size("fsdp")
    half = rank // 2
    anywhere = pl.BlockSpec(memory_space=pl.ANY)
    dma = pltpu.SemaphoreType.DMA
    results = pl.pallas_call(
        fused_kernel,
        out_shape=(
            jax.ShapeDtypeStruct(weight.shape, bf16),
            jax.ShapeDtypeStruct((own_rows, rank), f32),
            jax.ShapeDtypeStruct((own_rows, rank), f32),
        ),
        in_specs=[anywhere] * 6,
        out_specs=(anywhere,) * 3,
        scratch_shapes=[
            pltpu.VMEM(activations.shape, bf16),
            pltpu.VMEM(output_grads.shape, bf16),
            pltpu.VMEM((nf * ndp, own_rows, rank), bf16),
            pltpu.VMEM(weight.shape, bf16),
            pltpu.VMEM((own_rows, rank), f32),
            pltpu.VMEM((own_rows, rank), f32),
            pltpu.VMEM((ndp, own_rows, rank), bf16),
            pltpu.VMEM((nf, tokens // nf, rank), f32),
            pltpu.VMEM((nf, tokens // nf, rank), bf16),
            pltpu.VMEM((nf, tokens // nf, rank), bf16),
            pltpu.VMEM((nf, tokens // nf, rank), bf16),
            pltpu.VMEM((ndp, own_rows, rank), f32),
            pltpu.VMEM((ndp // 2, own_rows, rank), f32),
            pltpu.VMEM((2, own_rows, half), bf16),
            pltpu.VMEM((2, own_rows, half), bf16),
            pltpu.VMEM((2, own_rows, half), bf16),
            pltpu.VMEM((2, own_rows, half), bf16),
            pltpu.VMEM((own_rows, half), f32),
            pltpu.VMEM((own_rows, half), f32),
            pltpu.VMEM((own_rows, half), f32),
            pltpu.VMEM((own_rows, half), f32),
            dma((6,)), dma((6,)), dma((2,)), dma((3,)), dma((nf,)), dma((nf,)), dma((nf,)), dma((nf,)), dma((nf,)),
            dma((4,)), dma((4,)), dma((4,)), dma((4,)), dma((2,)), dma((2,)), dma((4, 8)), dma((4, 8)),
        ],
        compiler_params=pltpu.CompilerParams(
            collective_id=0, has_side_effects=True, vmem_limit_bytes=63 * 1024 * 1024
        ),
        cost_estimate=pl.CostEstimate(
            flops=2 * shard_rows * rank * (2 * tokens + nf * shard_rows), bytes_accessed=24 * 1024 * 1024, transcendentals=0
        ),
    )(
        activations, output_grads, basis.reshape(ndp, own_rows, rank), weight,
        first_moment, second_moment,
    )
    return pl.pallas_call(
        store_kernel,
        out_shape=[jax.ShapeDtypeStruct(r.shape, r.dtype) for r in results],
        in_specs=[anywhere] * 3,
        out_specs=[anywhere] * 3,
        scratch_shapes=[pltpu.VMEM(r.shape, r.dtype) for r in results] + [dma((18,)), dma((18,))],
        compiler_params=pltpu.CompilerParams(vmem_limit_bytes=63 * 1024 * 1024),
    )(*results)


def local(activations, output_grads, basis, weight, first_moment, second_moment):
    partial_product = jnp.dot(activations, basis, preferred_element_type=f32)
    projected = lax.psum(partial_product, "fsdp").astype(bf16)
    total_tokens = projected.shape[0] * lax.axis_size("dp")
    local_term = (
        lax.dot_general(
            output_grads, projected, (((0,), (0,)), ((), ())), preferred_element_type=f32
        )
        / total_tokens
    )
    low_grad = lax.psum_scatter(local_term, "dp", scatter_dimension=0, tiled=True)
    new_first, new_second, update = adam(first_moment, second_moment, low_grad)
    all_updates = lax.all_gather(update, "dp", axis=0, tiled=True)
    decoded = times_basis(all_updates, lax.all_gather(basis, "fsdp", axis=0, tiled=True))
    new_weight = (weight.astype(f32) - step_rate * decoded).astype(bf16)
    return (new_weight, new_first, new_second)


def solution(mesh):
    fused = mesh.shape["dp"] == 8 and mesh.shape["fsdp"] == 4
    return jax.shard_map(
        local_fused if fused else local,
        mesh=mesh,
        in_specs=(
            P("dp", "fsdp"),
            P("dp", "fsdp"),
            P("fsdp", None),
            P("fsdp", None),
            P(("fsdp", "dp"), None),
            P(("fsdp", "dp"), None),
        ),
        out_specs=(P("fsdp", None), P(("fsdp", "dp"), None), P(("fsdp", "dp"), None)),
        check_vma=False,
    )
```

```python
import functools

import jax
import jax.numpy as jnp
from jax import lax
from jax.experimental import pallas as pl
from jax.experimental.pallas import tpu as pltpu
from jax.sharding import PartitionSpec as P

first_decay = 0.9
second_decay = 0.999
first_fix = 1.0 - 0.9**10
second_fix = 1.0 - 0.999**10
step_rate = 0.01
tiny_eps = 1e-08
MESH = pl.DeviceIdType.MESH
f32 = jnp.float32
bf16 = jnp.bfloat16


def times_basis(update, rows):
    return lax.dot_general(update, rows, (((1,), (1,)), ((), ())), preferred_element_type=f32)


def adam(first, second, low_grad):
    new_first = first_decay * first + (1.0 - first_decay) * low_grad
    new_second = second_decay * second + (1.0 - second_decay) * low_grad * low_grad
    update = (new_first / first_fix / (jnp.sqrt(new_second / second_fix) + tiny_eps)).astype(bf16)
    return new_first, new_second, update


def fused_kernel(
    act_in, og_in, basis_in_ref, weight_in, first_in, second_in,
    weight_out, first_out, second_out,
    act, og, rows, weight, first, second, updates,
    part, part_send, part_recv, proj,
    grad, grad_core, sa1, sb1, ra1, rb1, sa2, sb2, ra2, rb2,
    load_sem, store_sem, z_send, z_fwd, z_recv, rs_send, rs_recv, ag_send, ag_recv,
    core_send, core_recv, h1_send, h1_recv, h2_send, h2_recv, pg_send, pg_recv,
):
    i = lax.axis_index("dp")
    j = lax.axis_index("fsdp")
    ndp, nf = 8, 4
    core, x, y = i % 2, (i // 2) % 2, i // 4
    sib = i + 1 - 2 * core
    xn = i + 2 * (1 - 2 * x)
    yn = i + 4 * (1 - 2 * y)
    dn = xn + 4 * (1 - 2 * y)
    tokens, rank = act.shape[0], first.shape[1]
    own_rows = first.shape[0]
    tb = tokens // nf
    total_tokens = tokens * ndp
    chunks = part.shape[0]
    width = rank // chunks
    lane = width // 2

    loads = [
        pltpu.make_async_copy(src, dst, load_sem.at[n])
        for n, (src, dst) in enumerate((
            (act_in, act),
            (basis_in_ref, rows.at[pl.ds(j * ndp, ndp)]),
            (og_in, og),
            (first_in, first),
            (second_in, second),
            (weight_in, weight),
        ))
    ]
    for load in loads:
        load.start()

    def remote(src, dst, ssem, rsem, dp, z):
        return pltpu.make_async_remote_copy(
            src_ref=src, dst_ref=dst, send_sem=ssem, recv_sem=rsem,
            device_id=(dp, z), device_id_type=MESH,
        )

    def got(dst, rsem, ssem):
        remote(dst, dst, ssem, rsem, sib, j).wait_recv()

    def sent(src, ssem, rsem):
        remote(src, src, ssem, rsem, sib, j).wait_send()

    barrier = pltpu.get_barrier_semaphore()
    for dp in (sib, xn, yn):
        pl.semaphore_signal(barrier, inc=1, device_id=(dp, j), device_id_type=MESH)
    for d in range(1, nf):
        pl.semaphore_signal(barrier, inc=1, device_id=(i, (j + d) % nf), device_id_type=MESH)
    pl.semaphore_wait(barrier, 3 + nf - 1)

    def z_piece(shard):
        return rows.at[shard * ndp + i]

    @pl.when(j < nf - 1)
    def _():
        remote(basis_in_ref.at[i], z_piece(j), z_send.at[0], z_recv.at[j], i, j + 1).start()

    @pl.when(j > 0)
    def _():
        remote(basis_in_ref.at[i], z_piece(j), z_send.at[1], z_recv.at[j], i, j - 1).start()

    loads[0].wait()
    loads[1].wait()

    def partial(c):
        acc = jnp.dot(
            act[...],
            rows[pl.ds(j * ndp, ndp), :, c * width : (c + 1) * width].reshape(ndp * own_rows, width),
            preferred_element_type=f32,
        ).reshape(nf, tb, width)
        part[c] = acc
        part_send[c] = acc.astype(bf16)

    def scatter(c):
        for d in (2, 1, 3):
            z = (j + d) % nf
            remote(part_send.at[c, z], part_recv.at[c, j], rs_send.at[c, z], rs_recv.at[c, j], i, z).start()

    def reduce_gather(c):
        total = part[c, j]
        for d in (1, 2, 3):
            z = (j + d) % nf
            got(part_recv.at[c, z], rs_recv.at[c, z], rs_send.at[c, z])
            total = total + part_recv[c, z].astype(f32)
        proj[c, j] = total.astype(bf16)
        for d in (2, 1, 3):
            z = (j + d) % nf
            remote(proj.at[c, j], proj.at[c, j], ag_send.at[c, z], ag_recv.at[c, j], i, z).start()

    partial(0)
    scatter(0)
    for c in range(1, chunks):
        partial(c)

    def columns(g, base, k, start, stop):
        if g < 3:
            return rows.at[base + k, :, pl.ds(rank * start // 2, rank * (stop - start) // 2)]
        return updates.at[k, :, pl.ds((g - 3) * width + lane * start, lane * (stop - start))]

    def block(g, base, k):
        return columns(g, base, k, 0, 2)

    def lane_a(g, base, k):
        return columns(g, base, k, 0, 1)

    def lane_b(g, base, k):
        return columns(g, base, k, 1, 2)

    def stage1(base, g):
        mine = block(g, base, i)
        remote(mine, mine, pg_send.at[g, 0], pg_recv.at[g, 0], xn, j).start()
        remote(mine, mine, pg_send.at[g, 1], pg_recv.at[g, 1], yn, j).start()
        remote(mine, mine, pg_send.at[g, 4], pg_recv.at[g, 4], sib, j).start()

    def stage2(base, g):
        bx, by = block(g, base, xn), block(g, base, yn)
        got(bx, pg_recv.at[g, 0], pg_send.at[g, 0])
        lb = lane_b(g, base, xn)
        remote(lb, lb, pg_send.at[g, 3], pg_recv.at[g, 3], yn, j).start()
        remote(bx, bx, pg_send.at[g, 5], pg_recv.at[g, 5], sib, j).start()
        got(by, pg_recv.at[g, 1], pg_send.at[g, 1])
        la = lane_a(g, base, yn)
        remote(la, la, pg_send.at[g, 2], pg_recv.at[g, 2], xn, j).start()
        remote(by, by, pg_send.at[g, 6], pg_recv.at[g, 6], sib, j).start()

    def stage3(base, g):
        got(lane_a(g, base, dn), pg_recv.at[g, 2], pg_send.at[g, 2])
        got(lane_b(g, base, dn), pg_recv.at[g, 3], pg_send.at[g, 3])
        bd = block(g, base, dn)
        remote(bd, bd, pg_send.at[g, 7], pg_recv.at[g, 7], sib, j).start()

    def stage4(base, g, receive=True):
        for q in range(4):
            o = (i, xn, yn, dn)[q]
            so = o + 1 - 2 * core
            if receive:
                got(block(g, base, so), pg_recv.at[g, 4 + q], pg_send.at[g, 4 + q])
            sent(block(g, base, o), pg_send.at[g, 4 + q], pg_recv.at[g, 4 + q])
        sent(block(g, base, i), pg_send.at[g, 0], pg_recv.at[g, 0])
        sent(block(g, base, i), pg_send.at[g, 1], pg_recv.at[g, 1])
        sent(lane_a(g, base, yn), pg_send.at[g, 2], pg_recv.at[g, 2])
        sent(lane_b(g, base, xn), pg_send.at[g, 3], pg_recv.at[g, 3])

    low = 1 - j // 2
    edge = low * j + (1 - low) * (nf - 1 - j)

    def shard_of(g):
        place = g + (g + nf - edge) // nf
        return low * place + (1 - low) * (nf - 1 - place)

    def basis_in(g):
        s = shard_of(g)
        got(z_piece(s), z_recv.at[s], z_send.at[0])

        @pl.when((s < j) & (j < nf - 1))
        def _():
            remote(z_piece(s), z_piece(s), z_fwd.at[g], z_recv.at[s], i, j + 1).start()

        @pl.when((s > j) & (j > 0))
        def _():
            remote(z_piece(s), z_piece(s), z_fwd.at[g], z_recv.at[s], i, j - 1).start()

        stage1(s * ndp, g)

    def basis_sent(g):
        s = shard_of(g)

        @pl.when(((s < j) & (j < nf - 1)) | ((s > j) & (j > 0)))
        def _():
            sent(z_piece(s), z_fwd.at[g], z_recv.at[s])

    mine = 2 * y + x
    order = (3 - mine, 2 * y + 1 - x, 2 * (1 - y) + x, mine)

    def low_grad(c):
        for d in (1, 2, 3):
            z = (j + d) % nf
            got(proj.at[c, z], ag_recv.at[c, z], ag_send.at[c, z])
        projected = proj[c].reshape(tokens, width)

        def term(k):
            cols = pl.ds(pl.multiple_of(k * own_rows, own_rows), own_rows)
            return lax.dot_general(
                og[:, cols], projected, (((0,), (0,)), ((), ())), preferred_element_type=f32
            )

        for q in range(4):
            grad[c, 4 + q] = term(2 * order[q] + 1 - core)
            remote(
                grad.at[c, 4 + q], grad_core.at[c, q], core_send.at[c, q], core_recv.at[c, q], sib, j
            ).start()
        for q in range(4):
            grad[c, q] = term(2 * order[q] + core)

    def hop1(c):
        for q in range(4):
            got(grad_core.at[c, q], core_recv.at[c, q], core_send.at[c, q])
            grad[c, q] = grad[c, q] + grad_core[c, q]
            if q in (0, 1):
                sa1[c, q] = grad[c, q, :, 0:lane].astype(bf16)
                remote(sa1.at[c, q], ra1.at[c, q], h1_send.at[c, q], h1_recv.at[c, q], xn, j).start()
            if q in (0, 2):
                n = q // 2
                sb1[c, n] = grad[c, q, :, lane:width].astype(bf16)
                remote(sb1.at[c, n], rb1.at[c, n], h1_send.at[c, 2 + n], h1_recv.at[c, 2 + n], yn, j).start()

    def hop2(c):
        got(ra1.at[c, 0], h1_recv.at[c, 0], h1_send.at[c, 0])
        sa2[c] = grad[c, 2, :, 0:lane] + ra1[c, 0].astype(f32)
        remote(sa2.at[c], ra2.at[c], h2_send.at[c, 0], h2_recv.at[c, 0], yn, j).start()
        got(rb1.at[c, 0], h1_recv.at[c, 2], h1_send.at[c, 2])
        sb2[c] = grad[c, 1, :, lane:width] + rb1[c, 0].astype(f32)
        remote(sb2.at[c], rb2.at[c], h2_send.at[c, 1], h2_recv.at[c, 1], xn, j).start()

    def step(c):
        got(ra1.at[c, 1], h1_recv.at[c, 1], h1_send.at[c, 1])
        got(rb1.at[c, 1], h1_recv.at[c, 3], h1_send.at[c, 3])
        for n, (r1, r2) in enumerate(((ra1, ra2), (rb1, rb2))):
            got(r2.at[c], h2_recv.at[c, n], h2_send.at[c, n])
            cols = pl.ds(c * width + n * lane, lane)
            summed = grad[c, 3, :, n * lane : (n + 1) * lane] + r1[c, 1].astype(f32) + r2[c]
            first[:, cols], second[:, cols], updates[i, :, cols] = adam(
                first[:, cols], second[:, cols], summed / total_tokens
            )
        stage1(0, 3 + c)

    middle = (j > 0) & (j < nf - 1)
    shard_base = [shard_of(g) * ndp for g in range(3)]
    basis_in(0)
    reduce_gather(0)
    scatter(1)
    basis_in(1)
    stage2(shard_base[0], 0)

    @pl.when(middle)
    def _():
        basis_in(2)

    reduce_gather(1)
    loads[2].wait()
    low_grad(0)
    hop1(0)
    stage3(shard_base[0], 0)
    stage2(shard_base[1], 1)
    hop2(0)

    @pl.when(jnp.logical_not(middle))
    def _():
        basis_in(2)

    low_grad(1)
    loads[3].wait()
    loads[4].wait()
    step(0)
    hop1(1)
    stage3(shard_base[1], 1)
    stage2(shard_base[2], 2)
    hop2(1)
    stage2(0, 3)
    stage3(shard_base[2], 2)
    step(1)
    stage3(0, 3)
    store_first = pltpu.make_async_copy(first, first_out, store_sem.at[4])
    store_second = pltpu.make_async_copy(second, second_out, store_sem.at[5])
    store_first.start()
    store_second.start()

    for g in range(3):
        stage4(shard_base[g], g)
        basis_sent(g)
    loads[5].wait()

    chunk = 4
    pair_rows = 2 * own_rows
    wide = chunk * own_rows

    def decode(n, o):
        pair = o // 2
        for g in range(3, 3 + chunks):
            got(block(g, 0, o + 1 - 2 * core), pg_recv.at[g, 4 + n], pg_send.at[g, 4 + n])
        left = updates[pl.ds(2 * pair, 2)].reshape(pair_rows, rank)
        at = pl.ds(pl.multiple_of(pair * pair_rows, pair_rows), pair_rows)

        def body(c, carry):
            cols = pl.ds(pl.multiple_of(c * wide, wide), wide)
            right = rows[pl.ds(c * chunk, chunk)].reshape(wide, rank)
            decoded = times_basis(left, right)
            weight[at, cols] = (weight[at, cols].astype(f32) - step_rate * decoded).astype(bf16)
            return carry

        lax.fori_loop(0, nf * ndp // chunk, body, 0)
        pltpu.make_async_copy(weight.at[at], weight_out.at[at], store_sem.at[n]).start()

    decode(0, i)
    stage2(0, 4)
    decode(1, xn)
    stage3(0, 4)
    decode(2, yn)
    decode(3, dn)
    stage4(0, 3, False)
    stage4(0, 4, False)

    @pl.when(j < nf - 1)
    def _():
        sent(basis_in_ref.at[i], z_send.at[0], z_recv.at[j])

    @pl.when(j > 0)
    def _():
        sent(basis_in_ref.at[i], z_send.at[1], z_recv.at[j])

    for c in range(chunks):
        for d in (1, 2, 3):
            z = (j + d) % nf
            sent(part_send.at[c, z], rs_send.at[c, z], rs_recv.at[c, z])
            sent(proj.at[c, j], ag_send.at[c, z], ag_recv.at[c, z])
        for q in range(4):
            sent(grad.at[c, 4 + q], core_send.at[c, q], core_recv.at[c, q])
        for n in range(2):
            sent(sa1.at[c, n], h1_send.at[c, n], h1_recv.at[c, n])
            sent(sb1.at[c, n], h1_send.at[c, 2 + n], h1_recv.at[c, 2 + n])
        sent(sa2.at[c], h2_send.at[c, 0], h2_recv.at[c, 0])
        sent(sb2.at[c], h2_send.at[c, 1], h2_recv.at[c, 1])
    store_first.wait()
    store_second.wait()
    for n, o in enumerate((i, xn, yn, dn)):
        at = pl.ds(pl.multiple_of(o // 2 * pair_rows, pair_rows), pair_rows)
        pltpu.make_async_copy(weight.at[at], weight_out.at[at], store_sem.at[n]).wait()


def store_kernel(
    weight, first, second, weight_out, first_out, second_out,
    weight_buf, first_buf, second_buf, in_sem, out_sem,
):
    pieces = 16
    size = weight.shape[0] // pieces
    parts = [
        (weight.at[pl.ds(k * size, size)], weight_buf.at[pl.ds(k * size, size)],
         weight_out.at[pl.ds(k * size, size)])
        for k in range(pieces)
    ] + [(first, first_buf, first_out), (second, second_buf, second_out)]
    ins = [pltpu.make_async_copy(a, b, in_sem.at[n]) for n, (a, b, _) in enumerate(parts)]
    outs = [pltpu.make_async_copy(b, c, out_sem.at[n]) for n, (_, b, c) in enumerate(parts)]
    for copy in ins:
        copy.start()
    for load, store in zip(ins, outs):
        load.wait()
        store.start()
    for copy in outs:
        copy.wait()


def local_fused(activations, output_grads, basis, weight, first_moment, second_moment):
    tokens, _ = activations.shape
    shard_rows, rank = basis.shape
    own_rows = first_moment.shape[0]
    ndp, nf = lax.axis_size("dp"), lax.axis_size("fsdp")
    chunks = 2
    width = rank // chunks
    anywhere = pl.BlockSpec(memory_space=pl.ANY)
    dma = pltpu.SemaphoreType.DMA
    results = pl.pallas_call(
        fused_kernel,
        out_shape=(
            jax.ShapeDtypeStruct(weight.shape, bf16),
            jax.ShapeDtypeStruct((own_rows, rank), f32),
            jax.ShapeDtypeStruct((own_rows, rank), f32),
        ),
        in_specs=[anywhere] * 6,
        out_specs=(anywhere,) * 3,
        scratch_shapes=[
            pltpu.VMEM(activations.shape, bf16),
            pltpu.VMEM(output_grads.shape, bf16),
            pltpu.VMEM((nf * ndp, own_rows, rank), bf16),
            pltpu.VMEM(weight.shape, bf16),
            pltpu.VMEM((own_rows, rank), f32),
            pltpu.VMEM((own_rows, rank), f32),
            pltpu.VMEM((ndp, own_rows, rank), bf16),
            pltpu.VMEM((chunks, nf, tokens // nf, width), f32),
            *[pltpu.VMEM((chunks, nf, tokens // nf, width), bf16)] * 3,
            pltpu.VMEM((chunks, ndp, own_rows, width), f32),
            pltpu.VMEM((chunks, ndp // 2, own_rows, width), f32),
            *[pltpu.VMEM((chunks, 2, own_rows, width // 2), bf16)] * 4,
            *[pltpu.VMEM((chunks, own_rows, width // 2), f32)] * 4,
            dma((6,)), dma((6,)), dma((2,)), dma((3,)), dma((nf,)), *[dma((chunks, nf))] * 4,
            *[dma((chunks, 4))] * 4, *[dma((chunks, 2))] * 2, *[dma((3 + chunks, 8))] * 2,
        ],
        compiler_params=pltpu.CompilerParams(
            collective_id=0, has_side_effects=True, vmem_limit_bytes=63 * 1024 * 1024
        ),
        cost_estimate=pl.CostEstimate(
            flops=2 * shard_rows * rank * (2 * tokens + nf * shard_rows), bytes_accessed=24 * 1024 * 1024, transcendentals=0
        ),
    )(
        activations, output_grads, basis.reshape(ndp, own_rows, rank), weight,
        first_moment, second_moment,
    )
    return pl.pallas_call(
        store_kernel,
        out_shape=[jax.ShapeDtypeStruct(r.shape, r.dtype) for r in results],
        in_specs=[anywhere] * 3,
        out_specs=[anywhere] * 3,
        scratch_shapes=[pltpu.VMEM(r.shape, r.dtype) for r in results] + [dma((18,)), dma((18,))],
        compiler_params=pltpu.CompilerParams(vmem_limit_bytes=63 * 1024 * 1024),
    )(*results)


def local(activations, output_grads, basis, weight, first_moment, second_moment):
    partial_product = jnp.dot(activations, basis, preferred_element_type=f32)
    projected = lax.psum(partial_product, "fsdp").astype(bf16)
    total_tokens = projected.shape[0] * lax.axis_size("dp")
    local_term = (
        lax.dot_general(
            output_grads, projected, (((0,), (0,)), ((), ())), preferred_element_type=f32
        )
        / total_tokens
    )
    low_grad = lax.psum_scatter(local_term, "dp", scatter_dimension=0, tiled=True)
    new_first, new_second, update = adam(first_moment, second_moment, low_grad)
    all_updates = lax.all_gather(update, "dp", axis=0, tiled=True)
    decoded = times_basis(all_updates, lax.all_gather(basis, "fsdp", axis=0, tiled=True))
    new_weight = (weight.astype(f32) - step_rate * decoded).astype(bf16)
    return (new_weight, new_first, new_second)


def solution(mesh):
    fused = mesh.shape["dp"] == 8 and mesh.shape["fsdp"] == 4
    return jax.shard_map(
        local_fused if fused else local,
        mesh=mesh,
        in_specs=(
            P("dp", "fsdp"),
            P("dp", "fsdp"),
            P("fsdp", None),
            P("fsdp", None),
            P(("fsdp", "dp"), None),
            P(("fsdp", "dp"), None),
        ),
        out_specs=(P("fsdp", None), P(("fsdp", "dp"), None), P(("fsdp", "dp"), None)),
        check_vma=False,
    )
```

```python
import functools

import jax
import jax.numpy as jnp
from jax import lax
from jax.experimental import pallas as pl
from jax.experimental.pallas import tpu as pltpu
from jax.sharding import PartitionSpec as P

first_decay = 0.9
second_decay = 0.999
first_fix = 1.0 - 0.9**10
second_fix = 1.0 - 0.999**10
step_rate = 0.01
tiny_eps = 1e-08
MESH = pl.DeviceIdType.MESH
f32 = jnp.float32
bf16 = jnp.bfloat16


def times_basis(update, rows):
    return lax.dot_general(update, rows, (((1,), (1,)), ((), ())), preferred_element_type=f32)


def adam(first, second, low_grad):
    new_first = first_decay * first + (1.0 - first_decay) * low_grad
    new_second = second_decay * second + (1.0 - second_decay) * low_grad * low_grad
    update = (new_first / first_fix / (jnp.sqrt(new_second / second_fix) + tiny_eps)).astype(bf16)
    return new_first, new_second, update


def fused_kernel(
    act_in, og_in, basis_in_ref, weight_in, first_in, second_in,
    weight_out, first_out, second_out,
    act, og, rows, weight, first, second, updates,
    part, part_send, part_recv, proj,
    grad, og_sib, proj_sib, sa1, sb1, ra1, rb1, sa2, sb2, ra2, rb2,
    load_sem, store_sem, z_send, z_fwd, z_recv, rs_send, rs_recv, ag_send, ag_recv,
    core_send, core_recv, og_send, og_recv, h1_send, h1_recv, h2_send, h2_recv, pg_send, pg_recv,
):
    i = lax.axis_index("dp")
    j = lax.axis_index("fsdp")
    ndp, nf = 8, 4
    core, x, y = i % 2, (i // 2) % 2, i // 4
    sib = i + 1 - 2 * core
    xn = i + 2 * (1 - 2 * x)
    yn = i + 4 * (1 - 2 * y)
    dn = xn + 4 * (1 - 2 * y)
    tokens, rank = act.shape[0], first.shape[1]
    own_rows = first.shape[0]
    tb = tokens // nf
    half = rank // 2
    total_tokens = tokens * ndp

    loads = [
        pltpu.make_async_copy(src, dst, load_sem.at[n])
        for n, (src, dst) in enumerate((
            (act_in, act),
            (basis_in_ref, rows.at[pl.ds(j * ndp, ndp)]),
            (og_in, og),
            (first_in, first),
            (second_in, second),
            (weight_in, weight),
        ))
    ]
    for load in loads:
        load.start()

    def remote(src, dst, ssem, rsem, dp, z):
        return pltpu.make_async_remote_copy(
            src_ref=src, dst_ref=dst, send_sem=ssem, recv_sem=rsem,
            device_id=(dp, z), device_id_type=MESH,
        )

    def got(dst, rsem, ssem):
        remote(dst, dst, ssem, rsem, sib, j).wait_recv()

    def sent(src, ssem, rsem):
        remote(src, src, ssem, rsem, sib, j).wait_send()

    barrier = pltpu.get_barrier_semaphore()
    for dp in (sib, xn, yn):
        pl.semaphore_signal(barrier, inc=1, device_id=(dp, j), device_id_type=MESH)
    for d in range(1, nf):
        pl.semaphore_signal(barrier, inc=1, device_id=(i, (j + d) % nf), device_id_type=MESH)
    pl.semaphore_wait(barrier, 3 + nf - 1)

    mine = 2 * y + x
    order = (3 - mine, 2 * y + 1 - x, 2 * (1 - y) + x, mine)

    def z_piece(shard):
        return rows.at[shard * ndp + i]

    @pl.when(j < nf - 1)
    def _():
        remote(basis_in_ref.at[i], z_piece(j), z_send.at[0], z_recv.at[j], i, j + 1).start()

    @pl.when(j > 0)
    def _():
        remote(basis_in_ref.at[i], z_piece(j), z_send.at[1], z_recv.at[j], i, j - 1).start()

    def og_columns(k):
        return pl.ds(pl.multiple_of(k * own_rows, own_rows), own_rows)

    for q in range(4):
        remote(
            og_in.at[:, og_columns(2 * order[q] + 1 - core)], og_sib.at[q],
            og_send.at[q], og_recv.at[q], sib, j,
        ).start()

    loads[0].wait()
    loads[1].wait()
    acc = jnp.dot(
        act[...],
        rows[pl.ds(j * ndp, ndp)].reshape(ndp * own_rows, rank),
        preferred_element_type=f32,
    )
    part[...] = acc.reshape(nf, tb, rank)
    part_send[...] = acc.reshape(nf, tb, rank).astype(bf16)
    for d in (1, 2, 3):
        z = (j + d) % nf
        remote(part_send.at[z], part_recv.at[j], rs_send.at[z], rs_recv.at[j], i, z).start()

    def block(buf, base, k):
        return buf.at[base + k]

    def lane_a(buf, base, k):
        return buf.at[base + k, :, pl.ds(0, half)]

    def lane_b(buf, base, k):
        return buf.at[base + k, :, pl.ds(half, half)]

    def stage1(buf, base, g):
        mine = block(buf, base, i)
        remote(mine, mine, pg_send.at[g, 0], pg_recv.at[g, 0], xn, j).start()
        remote(mine, mine, pg_send.at[g, 1], pg_recv.at[g, 1], yn, j).start()
        remote(mine, mine, pg_send.at[g, 4], pg_recv.at[g, 4], sib, j).start()

    def stage2(buf, base, g):
        bx, by = block(buf, base, xn), block(buf, base, yn)
        got(bx, pg_recv.at[g, 0], pg_send.at[g, 0])
        lb = lane_b(buf, base, xn)
        remote(lb, lb, pg_send.at[g, 3], pg_recv.at[g, 3], yn, j).start()
        remote(bx, bx, pg_send.at[g, 5], pg_recv.at[g, 5], sib, j).start()
        got(by, pg_recv.at[g, 1], pg_send.at[g, 1])
        la = lane_a(buf, base, yn)
        remote(la, la, pg_send.at[g, 2], pg_recv.at[g, 2], xn, j).start()
        remote(by, by, pg_send.at[g, 6], pg_recv.at[g, 6], sib, j).start()

    def stage3(buf, base, g):
        got(lane_a(buf, base, dn), pg_recv.at[g, 2], pg_send.at[g, 2])
        got(lane_b(buf, base, dn), pg_recv.at[g, 3], pg_send.at[g, 3])
        bd = block(buf, base, dn)
        remote(bd, bd, pg_send.at[g, 7], pg_recv.at[g, 7], sib, j).start()

    def stage4(buf, base, g, receive=True):
        for q in range(4):
            o = (i, xn, yn, dn)[q]
            so = o + 1 - 2 * core
            if receive:
                got(block(buf, base, so), pg_recv.at[g, 4 + q], pg_send.at[g, 4 + q])
            sent(block(buf, base, o), pg_send.at[g, 4 + q], pg_recv.at[g, 4 + q])
        sent(block(buf, base, i), pg_send.at[g, 0], pg_recv.at[g, 0])
        sent(block(buf, base, i), pg_send.at[g, 1], pg_recv.at[g, 1])
        sent(lane_a(buf, base, yn), pg_send.at[g, 2], pg_recv.at[g, 2])
        sent(lane_b(buf, base, xn), pg_send.at[g, 3], pg_recv.at[g, 3])

    low = 1 - j // 2
    edge = low * j + (1 - low) * (nf - 1 - j)

    def shard_of(g):
        place = g + (g + nf - edge) // nf
        return low * place + (1 - low) * (nf - 1 - place)

    def basis_in(g):
        s = shard_of(g)
        got(z_piece(s), z_recv.at[s], z_send.at[0])

        @pl.when((s < j) & (j < nf - 1))
        def _():
            remote(z_piece(s), z_piece(s), z_fwd.at[g], z_recv.at[s], i, j + 1).start()

        @pl.when((s > j) & (j > 0))
        def _():
            remote(z_piece(s), z_piece(s), z_fwd.at[g], z_recv.at[s], i, j - 1).start()

        stage1(rows, s * ndp, g)

    def basis_sent(g):
        s = shard_of(g)

        @pl.when(((s < j) & (j < nf - 1)) | ((s > j) & (j > 0)))
        def _():
            sent(z_piece(s), z_fwd.at[g], z_recv.at[s])

    basis_in(0)
    basis_in(1)

    total = part[j]
    for d in (1, 2, 3):
        z = (j + d) % nf
        got(part_recv.at[z], rs_recv.at[z], rs_send.at[z])
        total = total + part_recv[z].astype(f32)
    proj[j] = total.astype(bf16)
    for d in (1, 2, 3):
        z = (j + d) % nf
        remote(proj.at[j], proj.at[j], ag_send.at[z], ag_recv.at[j], i, z).start()
    remote(proj.at[j], proj_sib.at[j], core_send.at[j], core_recv.at[j], sib, j).start()

    stage2(rows, shard_of(0) * ndp, 0)
    basis_in(2)
    stage3(rows, shard_of(0) * ndp, 0)
    stage2(rows, shard_of(1) * ndp, 1)

    for d in (1, 2, 3):
        z = (j + d) % nf
        got(proj.at[z], ag_recv.at[z], ag_send.at[z])
        remote(proj.at[z], proj_sib.at[z], core_send.at[z], core_recv.at[z], sib, j).start()

    loads[2].wait()
    projected = proj[...].reshape(tokens, rank)

    def over_tokens(left, right):
        return lax.dot_general(left, right, (((0,), (0,)), ((), ())), preferred_element_type=f32)

    for q in range(4):
        grad[q] = over_tokens(og[:, og_columns(2 * order[q] + core)], projected)
    for q in range(4):
        got(og_sib.at[q], og_recv.at[q], og_send.at[q])
    for z in range(nf):
        got(proj_sib.at[z], core_recv.at[z], core_send.at[z])
    projected_sib = proj_sib[...].reshape(tokens, rank)

    for q in range(4):
        grad[q] = grad[q] + over_tokens(og_sib[q], projected_sib)
        if q in (0, 1):
            sa1[q] = grad[q, :, 0:half].astype(bf16)
            remote(sa1.at[q], ra1.at[q], h1_send.at[q], h1_recv.at[q], xn, j).start()
        if q in (0, 2):
            n = q // 2
            sb1[n] = grad[q, :, half:rank].astype(bf16)
            remote(sb1.at[n], rb1.at[n], h1_send.at[2 + n], h1_recv.at[2 + n], yn, j).start()
    stage3(rows, shard_of(1) * ndp, 1)
    stage2(rows, shard_of(2) * ndp, 2)
    got(ra1.at[0], h1_recv.at[0], h1_send.at[0])
    sa2[...] = grad[2, :, 0:half] + ra1[0].astype(f32)
    remote(sa2, ra2, h2_send.at[0], h2_recv.at[0], yn, j).start()
    got(rb1.at[0], h1_recv.at[2], h1_send.at[2])
    sb2[...] = grad[1, :, half:rank] + rb1[0].astype(f32)
    remote(sb2, rb2, h2_send.at[1], h2_recv.at[1], xn, j).start()
    got(ra1.at[1], h1_recv.at[1], h1_send.at[1])
    got(rb1.at[1], h1_recv.at[3], h1_send.at[3])

    stage3(rows, shard_of(2) * ndp, 2)
    loads[3].wait()
    loads[4].wait()
    got(ra2, h2_recv.at[0], h2_send.at[0])
    nf_a, ns_a, up_a = adam(
        first[:, 0:half], second[:, 0:half], (grad[3, :, 0:half] + ra1[1].astype(f32) + ra2[...]) / total_tokens
    )
    first[:, 0:half] = nf_a
    second[:, 0:half] = ns_a
    updates[i, :, 0:half] = up_a
    got(rb2, h2_recv.at[1], h2_send.at[1])
    nf_b, ns_b, up_b = adam(
        first[:, half:rank], second[:, half:rank], (grad[3, :, half:rank] + rb1[1].astype(f32) + rb2[...]) / total_tokens
    )
    first[:, half:rank] = nf_b
    second[:, half:rank] = ns_b
    updates[i, :, half:rank] = up_b
    stage1(updates, 0, 3)

    store_first = pltpu.make_async_copy(first, first_out, store_sem.at[4])
    store_second = pltpu.make_async_copy(second, second_out, store_sem.at[5])
    store_first.start()
    store_second.start()

    for g in range(3):
        stage4(rows, shard_of(g) * ndp, g)
        basis_sent(g)
    loads[5].wait()

    chunk = 4
    pair_rows = 2 * own_rows
    wide = chunk * own_rows

    def decode(n, o):
        pair = o // 2
        got(block(updates, 0, o + 1 - 2 * core), pg_recv.at[3, 4 + n], pg_send.at[3, 4 + n])
        left = updates[pl.ds(2 * pair, 2)].reshape(pair_rows, rank)
        at = pl.ds(pl.multiple_of(pair * pair_rows, pair_rows), pair_rows)

        def body(c, carry):
            cols = pl.ds(pl.multiple_of(c * wide, wide), wide)
            right = rows[pl.ds(c * chunk, chunk)].reshape(wide, rank)
            decoded = times_basis(left, right)
            weight[at, cols] = (weight[at, cols].astype(f32) - step_rate * decoded).astype(bf16)
            return carry

        lax.fori_loop(0, nf * ndp // chunk, body, 0)
        pltpu.make_async_copy(weight.at[at], weight_out.at[at], store_sem.at[n]).start()

    decode(0, i)
    stage2(updates, 0, 3)
    decode(1, xn)
    stage3(updates, 0, 3)
    decode(2, yn)
    decode(3, dn)
    stage4(updates, 0, 3, False)

    @pl.when(j < nf - 1)
    def _():
        sent(basis_in_ref.at[i], z_send.at[0], z_recv.at[j])

    @pl.when(j > 0)
    def _():
        sent(basis_in_ref.at[i], z_send.at[1], z_recv.at[j])

    for d in (1, 2, 3):
        z = (j + d) % nf
        sent(part_send.at[z], rs_send.at[z], rs_recv.at[z])
        sent(proj.at[j], ag_send.at[z], ag_recv.at[z])
    for q in range(4):
        sent(proj.at[q], core_send.at[q], core_recv.at[q])
        sent(og_sib.at[q], og_send.at[q], og_recv.at[q])
    for n in range(2):
        sent(sa1.at[n], h1_send.at[n], h1_recv.at[n])
        sent(sb1.at[n], h1_send.at[2 + n], h1_recv.at[2 + n])
    sent(sa2, h2_send.at[0], h2_recv.at[0])
    sent(sb2, h2_send.at[1], h2_recv.at[1])
    store_first.wait()
    store_second.wait()
    for n, o in enumerate((i, xn, yn, dn)):
        at = pl.ds(pl.multiple_of(o // 2 * pair_rows, pair_rows), pair_rows)
        pltpu.make_async_copy(weight.at[at], weight_out.at[at], store_sem.at[n]).wait()


def store_kernel(
    weight, first, second, weight_out, first_out, second_out,
    weight_buf, first_buf, second_buf, in_sem, out_sem,
):
    pieces = 16
    size = weight.shape[0] // pieces
    parts = [
        (weight.at[pl.ds(k * size, size)], weight_buf.at[pl.ds(k * size, size)],
         weight_out.at[pl.ds(k * size, size)])
        for k in range(pieces)
    ] + [(first, first_buf, first_out), (second, second_buf, second_out)]
    ins = [pltpu.make_async_copy(a, b, in_sem.at[n]) for n, (a, b, _) in enumerate(parts)]
    outs = [pltpu.make_async_copy(b, c, out_sem.at[n]) for n, (_, b, c) in enumerate(parts)]
    for copy in ins:
        copy.start()
    for load, store in zip(ins, outs):
        load.wait()
        store.start()
    for copy in outs:
        copy.wait()


def local_fused(activations, output_grads, basis, weight, first_moment, second_moment):
    tokens, _ = activations.shape
    shard_rows, rank = basis.shape
    own_rows = first_moment.shape[0]
    ndp, nf = lax.axis_size("dp"), lax.axis_size("fsdp")
    half = rank // 2
    anywhere = pl.BlockSpec(memory_space=pl.ANY)
    dma = pltpu.SemaphoreType.DMA
    results = pl.pallas_call(
        fused_kernel,
        out_shape=(
            jax.ShapeDtypeStruct(weight.shape, bf16),
            jax.ShapeDtypeStruct((own_rows, rank), f32),
            jax.ShapeDtypeStruct((own_rows, rank), f32),
        ),
        in_specs=[anywhere] * 6,
        out_specs=(anywhere,) * 3,
        scratch_shapes=[
            pltpu.VMEM(activations.shape, bf16),
            pltpu.VMEM(output_grads.shape, bf16),
            pltpu.VMEM((nf * ndp, own_rows, rank), bf16),
            pltpu.VMEM(weight.shape, bf16),
            pltpu.VMEM((own_rows, rank), f32),
            pltpu.VMEM((own_rows, rank), f32),
            pltpu.VMEM((ndp, own_rows, rank), bf16),
            pltpu.VMEM((nf, tokens // nf, rank), f32),
            pltpu.VMEM((nf, tokens // nf, rank), bf16),
            pltpu.VMEM((nf, tokens // nf, rank), bf16),
            pltpu.VMEM((nf, tokens // nf, rank), bf16),
            pltpu.VMEM((ndp // 2, own_rows, rank), f32),
            pltpu.VMEM((ndp // 2, tokens, own_rows), bf16),
            pltpu.VMEM((nf, tokens // nf, rank), bf16),
            pltpu.VMEM((2, own_rows, half), bf16),
            pltpu.VMEM((2, own_rows, half), bf16),
            pltpu.VMEM((2, own_rows, half), bf16),
            pltpu.VMEM((2, own_rows, half), bf16),
            pltpu.VMEM((own_rows, half), f32),
            pltpu.VMEM((own_rows, half), f32),
            pltpu.VMEM((own_rows, half), f32),
            pltpu.VMEM((own_rows, half), f32),
            dma((6,)), dma((6,)), dma((2,)), dma((3,)), dma((nf,)), dma((nf,)), dma((nf,)), dma((nf,)), dma((nf,)),
            *[dma((4,))] * 6, dma((2,)), dma((2,)), dma((4, 8)), dma((4, 8)),
        ],
        compiler_params=pltpu.CompilerParams(
            collective_id=0, has_side_effects=True, vmem_limit_bytes=63 * 1024 * 1024
        ),
        cost_estimate=pl.CostEstimate(
            flops=2 * shard_rows * rank * (2 * tokens + nf * shard_rows), bytes_accessed=24 * 1024 * 1024, transcendentals=0
        ),
    )(
        activations, output_grads, basis.reshape(ndp, own_rows, rank), weight,
        first_moment, second_moment,
    )
    return pl.pallas_call(
        store_kernel,
        out_shape=[jax.ShapeDtypeStruct(r.shape, r.dtype) for r in results],
        in_specs=[anywhere] * 3,
        out_specs=[anywhere] * 3,
        scratch_shapes=[pltpu.VMEM(r.shape, r.dtype) for r in results] + [dma((18,)), dma((18,))],
        compiler_params=pltpu.CompilerParams(vmem_limit_bytes=63 * 1024 * 1024),
    )(*results)


def local(activations, output_grads, basis, weight, first_moment, second_moment):
    partial_product = jnp.dot(activations, basis, preferred_element_type=f32)
    projected = lax.psum(partial_product, "fsdp").astype(bf16)
    total_tokens = projected.shape[0] * lax.axis_size("dp")
    local_term = (
        lax.dot_general(
            output_grads, projected, (((0,), (0,)), ((), ())), preferred_element_type=f32
        )
        / total_tokens
    )
    low_grad = lax.psum_scatter(local_term, "dp", scatter_dimension=0, tiled=True)
    new_first, new_second, update = adam(first_moment, second_moment, low_grad)
    all_updates = lax.all_gather(update, "dp", axis=0, tiled=True)
    decoded = times_basis(all_updates, lax.all_gather(basis, "fsdp", axis=0, tiled=True))
    new_weight = (weight.astype(f32) - step_rate * decoded).astype(bf16)
    return (new_weight, new_first, new_second)


def solution(mesh):
    fused = mesh.shape["dp"] == 8 and mesh.shape["fsdp"] == 4
    return jax.shard_map(
        local_fused if fused else local,
        mesh=mesh,
        in_specs=(
            P("dp", "fsdp"),
            P("dp", "fsdp"),
            P("fsdp", None),
            P("fsdp", None),
            P(("fsdp", "dp"), None),
            P(("fsdp", "dp"), None),
        ),
        out_specs=(P("fsdp", None), P(("fsdp", "dp"), None), P(("fsdp", "dp"), None)),
        check_vma=False,
    )
```

```python
import functools

import jax
import jax.numpy as jnp
from jax import lax
from jax.experimental import pallas as pl
from jax.experimental.pallas import tpu as pltpu
from jax.sharding import PartitionSpec as P

first_decay = 0.9
second_decay = 0.999
first_fix = 1.0 - 0.9**10
second_fix = 1.0 - 0.999**10
step_rate = 0.01
tiny_eps = 1e-08
MESH = pl.DeviceIdType.MESH
f32 = jnp.float32
bf16 = jnp.bfloat16


def times_basis(update, rows):
    return lax.dot_general(update, rows, (((1,), (1,)), ((), ())), preferred_element_type=f32)


def adam(first, second, low_grad):
    new_first = first_decay * first + (1.0 - first_decay) * low_grad
    new_second = second_decay * second + (1.0 - second_decay) * low_grad * low_grad
    update = (new_first / first_fix / (jnp.sqrt(new_second / second_fix) + tiny_eps)).astype(bf16)
    return new_first, new_second, update


def fused_kernel(
    act_in, og_in, basis_in_ref, weight_in, first_in, second_in,
    weight_out, first_out, second_out,
    act, og, rows, weight, first, second, updates,
    part, part_send, part_recv, proj,
    grad, og_sib, proj_sib, sa1, sb1, ra1, rb1, sa2, sb2, ra2, rb2,
    load_sem, store_sem, z_send, z_fwd, z_recv, rs_send, rs_recv, ag_send, ag_recv,
    core_send, core_recv, og_send, og_recv, h1_send, h1_recv, h2_send, h2_recv, pg_send, pg_recv,
):
    i = lax.axis_index("dp")
    j = lax.axis_index("fsdp")
    ndp, nf = 8, 4
    core, x, y = i % 2, (i // 2) % 2, i // 4
    sib = i + 1 - 2 * core
    xn = i + 2 * (1 - 2 * x)
    yn = i + 4 * (1 - 2 * y)
    dn = xn + 4 * (1 - 2 * y)
    tokens, rank = act.shape[0], first.shape[1]
    own_rows = first.shape[0]
    tb = tokens // nf
    half = rank // 2
    total_tokens = tokens * ndp

    loads = [
        pltpu.make_async_copy(src, dst, load_sem.at[n])
        for n, (src, dst) in enumerate((
            (act_in, act),
            (basis_in_ref, rows.at[pl.ds(j * ndp, ndp)]),
            (og_in, og),
            (first_in, first),
            (second_in, second),
            (weight_in, weight),
        ))
    ]
    for load in loads:
        load.start()

    def remote(src, dst, ssem, rsem, dp, z):
        return pltpu.make_async_remote_copy(
            src_ref=src, dst_ref=dst, send_sem=ssem, recv_sem=rsem,
            device_id=(dp, z), device_id_type=MESH,
        )

    def got(dst, rsem, ssem):
        remote(dst, dst, ssem, rsem, sib, j).wait_recv()

    def sent(src, ssem, rsem):
        remote(src, src, ssem, rsem, sib, j).wait_send()

    barrier = pltpu.get_barrier_semaphore()
    for dp in (sib, xn, yn):
        pl.semaphore_signal(barrier, inc=1, device_id=(dp, j), device_id_type=MESH)
    for d in range(1, nf):
        pl.semaphore_signal(barrier, inc=1, device_id=(i, (j + d) % nf), device_id_type=MESH)
    pl.semaphore_wait(barrier, 3 + nf - 1)

    mine = 2 * y + x
    order = (3 - mine, 2 * y + 1 - x, 2 * (1 - y) + x, mine)

    def z_piece(shard):
        return rows.at[shard * ndp + i]

    @pl.when(j < nf - 1)
    def _():
        remote(basis_in_ref.at[i], z_piece(j), z_send.at[0], z_recv.at[j], i, j + 1).start()

    @pl.when(j > 0)
    def _():
        remote(basis_in_ref.at[i], z_piece(j), z_send.at[1], z_recv.at[j], i, j - 1).start()

    def og_columns(k):
        return pl.ds(pl.multiple_of(k * own_rows, own_rows), own_rows)

    for q in range(4):
        remote(
            og_in.at[:, og_columns(2 * order[q] + 1 - core)], og_sib.at[q],
            og_send.at[q], og_recv.at[q], sib, j,
        ).start()

    loads[0].wait()
    loads[1].wait()
    acc = jnp.dot(
        act[...],
        rows[pl.ds(j * ndp, ndp)].reshape(ndp * own_rows, rank),
        preferred_element_type=f32,
    )
    part[...] = acc.reshape(nf, tb, rank)
    part_send[...] = acc.reshape(nf, tb, rank).astype(bf16)
    def scatter():
        for d in (2, 1, 3):
            z = (j + d) % nf
            remote(part_send.at[z], part_recv.at[j], rs_send.at[z], rs_recv.at[j], i, z).start()

    def block(buf, base, k):
        return buf.at[base + k]

    def lane_a(buf, base, k):
        return buf.at[base + k, :, pl.ds(0, half)]

    def lane_b(buf, base, k):
        return buf.at[base + k, :, pl.ds(half, half)]

    def stage1(buf, base, g):
        mine = block(buf, base, i)
        remote(mine, mine, pg_send.at[g, 0], pg_recv.at[g, 0], xn, j).start()
        remote(mine, mine, pg_send.at[g, 1], pg_recv.at[g, 1], yn, j).start()
        remote(mine, mine, pg_send.at[g, 4], pg_recv.at[g, 4], sib, j).start()

    def stage2(buf, base, g):
        bx, by = block(buf, base, xn), block(buf, base, yn)
        got(bx, pg_recv.at[g, 0], pg_send.at[g, 0])
        lb = lane_b(buf, base, xn)
        remote(lb, lb, pg_send.at[g, 3], pg_recv.at[g, 3], yn, j).start()
        remote(bx, bx, pg_send.at[g, 5], pg_recv.at[g, 5], sib, j).start()
        got(by, pg_recv.at[g, 1], pg_send.at[g, 1])
        la = lane_a(buf, base, yn)
        remote(la, la, pg_send.at[g, 2], pg_recv.at[g, 2], xn, j).start()
        remote(by, by, pg_send.at[g, 6], pg_recv.at[g, 6], sib, j).start()

    def stage3(buf, base, g):
        got(lane_a(buf, base, dn), pg_recv.at[g, 2], pg_send.at[g, 2])
        got(lane_b(buf, base, dn), pg_recv.at[g, 3], pg_send.at[g, 3])
        bd = block(buf, base, dn)
        remote(bd, bd, pg_send.at[g, 7], pg_recv.at[g, 7], sib, j).start()

    def stage4(buf, base, g, receive=True):
        for q in range(4):
            o = (i, xn, yn, dn)[q]
            so = o + 1 - 2 * core
            if receive:
                got(block(buf, base, so), pg_recv.at[g, 4 + q], pg_send.at[g, 4 + q])
            sent(block(buf, base, o), pg_send.at[g, 4 + q], pg_recv.at[g, 4 + q])
        sent(block(buf, base, i), pg_send.at[g, 0], pg_recv.at[g, 0])
        sent(block(buf, base, i), pg_send.at[g, 1], pg_recv.at[g, 1])
        sent(lane_a(buf, base, yn), pg_send.at[g, 2], pg_recv.at[g, 2])
        sent(lane_b(buf, base, xn), pg_send.at[g, 3], pg_recv.at[g, 3])

    low = 1 - j // 2
    edge = low * j + (1 - low) * (nf - 1 - j)

    def shard_of(g):
        place = g + (g + nf - edge) // nf
        return low * place + (1 - low) * (nf - 1 - place)

    def basis_in(g):
        s = shard_of(g)
        got(z_piece(s), z_recv.at[s], z_send.at[0])

        @pl.when((s < j) & (j < nf - 1))
        def _():
            remote(z_piece(s), z_piece(s), z_fwd.at[g], z_recv.at[s], i, j + 1).start()

        @pl.when((s > j) & (j > 0))
        def _():
            remote(z_piece(s), z_piece(s), z_fwd.at[g], z_recv.at[s], i, j - 1).start()

        stage1(rows, s * ndp, g)

    def basis_sent(g):
        s = shard_of(g)

        @pl.when(((s < j) & (j < nf - 1)) | ((s > j) & (j > 0)))
        def _():
            sent(z_piece(s), z_fwd.at[g], z_recv.at[s])

    middle = (j > 0) & (j < nf - 1)

    @pl.when(jnp.logical_not(middle))
    def _():
        scatter()

    basis_in(0)
    basis_in(1)

    @pl.when(middle)
    def _():
        scatter()
        basis_in(2)

    stage2(rows, shard_of(0) * ndp, 0)

    total = part[j]
    for d in (1, 2, 3):
        z = (j + d) % nf
        got(part_recv.at[z], rs_recv.at[z], rs_send.at[z])
        total = total + part_recv[z].astype(f32)
    proj[j] = total.astype(bf16)
    for d in (1, 2, 3):
        z = (j + d) % nf
        remote(proj.at[j], proj.at[j], ag_send.at[z], ag_recv.at[j], i, z).start()
    remote(proj.at[j], proj_sib.at[j], core_send.at[j], core_recv.at[j], sib, j).start()

    @pl.when(jnp.logical_not(middle))
    def _():
        basis_in(2)

    stage3(rows, shard_of(0) * ndp, 0)
    stage2(rows, shard_of(1) * ndp, 1)

    for d in (1, 2, 3):
        z = (j + d) % nf
        got(proj.at[z], ag_recv.at[z], ag_send.at[z])
        remote(proj.at[z], proj_sib.at[z], core_send.at[z], core_recv.at[z], sib, j).start()

    loads[2].wait()
    projected = proj[...].reshape(tokens, rank)

    def over_tokens(left, right):
        return lax.dot_general(left, right, (((0,), (0,)), ((), ())), preferred_element_type=f32)

    for q in range(4):
        grad[q] = over_tokens(og[:, og_columns(2 * order[q] + core)], projected)
    stage3(rows, shard_of(1) * ndp, 1)
    stage2(rows, shard_of(2) * ndp, 2)
    for q in range(4):
        got(og_sib.at[q], og_recv.at[q], og_send.at[q])
    for z in range(nf):
        got(proj_sib.at[z], core_recv.at[z], core_send.at[z])
    projected_sib = proj_sib[...].reshape(tokens, rank)

    for q in range(4):
        grad[q] = grad[q] + over_tokens(og_sib[q], projected_sib)
        if q in (0, 1):
            sa1[q] = grad[q, :, 0:half].astype(bf16)
            remote(sa1.at[q], ra1.at[q], h1_send.at[q], h1_recv.at[q], xn, j).start()
        if q in (0, 2):
            n = q // 2
            sb1[n] = grad[q, :, half:rank].astype(bf16)
            remote(sb1.at[n], rb1.at[n], h1_send.at[2 + n], h1_recv.at[2 + n], yn, j).start()
    got(ra1.at[0], h1_recv.at[0], h1_send.at[0])
    sa2[...] = grad[2, :, 0:half] + ra1[0].astype(f32)
    remote(sa2, ra2, h2_send.at[0], h2_recv.at[0], yn, j).start()
    got(rb1.at[0], h1_recv.at[2], h1_send.at[2])
    sb2[...] = grad[1, :, half:rank] + rb1[0].astype(f32)
    remote(sb2, rb2, h2_send.at[1], h2_recv.at[1], xn, j).start()
    got(ra1.at[1], h1_recv.at[1], h1_send.at[1])
    got(rb1.at[1], h1_recv.at[3], h1_send.at[3])

    stage3(rows, shard_of(2) * ndp, 2)
    loads[3].wait()
    loads[4].wait()
    got(ra2, h2_recv.at[0], h2_send.at[0])
    nf_a, ns_a, up_a = adam(
        first[:, 0:half], second[:, 0:half], (grad[3, :, 0:half] + ra1[1].astype(f32) + ra2[...]) / total_tokens
    )
    first[:, 0:half] = nf_a
    second[:, 0:half] = ns_a
    updates[i, :, 0:half] = up_a
    got(rb2, h2_recv.at[1], h2_send.at[1])
    nf_b, ns_b, up_b = adam(
        first[:, half:rank], second[:, half:rank], (grad[3, :, half:rank] + rb1[1].astype(f32) + rb2[...]) / total_tokens
    )
    first[:, half:rank] = nf_b
    second[:, half:rank] = ns_b
    updates[i, :, half:rank] = up_b
    stage1(updates, 0, 3)

    store_first = pltpu.make_async_copy(first, first_out, store_sem.at[4])
    store_second = pltpu.make_async_copy(second, second_out, store_sem.at[5])
    store_first.start()
    store_second.start()

    for g in range(3):
        stage4(rows, shard_of(g) * ndp, g)
        basis_sent(g)
    loads[5].wait()

    chunk = 4
    pair_rows = 2 * own_rows
    wide = chunk * own_rows

    def decode(n, o):
        pair = o // 2
        got(block(updates, 0, o + 1 - 2 * core), pg_recv.at[3, 4 + n], pg_send.at[3, 4 + n])
        left = updates[pl.ds(2 * pair, 2)].reshape(pair_rows, rank)
        at = pl.ds(pl.multiple_of(pair * pair_rows, pair_rows), pair_rows)

        def body(c, carry):
            cols = pl.ds(pl.multiple_of(c * wide, wide), wide)
            right = rows[pl.ds(c * chunk, chunk)].reshape(wide, rank)
            decoded = times_basis(left, right)
            weight[at, cols] = (weight[at, cols].astype(f32) - step_rate * decoded).astype(bf16)
            return carry

        lax.fori_loop(0, nf * ndp // chunk, body, 0)
        pltpu.make_async_copy(weight.at[at], weight_out.at[at], store_sem.at[n]).start()

    decode(0, i)
    stage2(updates, 0, 3)
    decode(1, xn)
    stage3(updates, 0, 3)
    decode(2, yn)
    decode(3, dn)
    stage4(updates, 0, 3, False)

    @pl.when(j < nf - 1)
    def _():
        sent(basis_in_ref.at[i], z_send.at[0], z_recv.at[j])

    @pl.when(j > 0)
    def _():
        sent(basis_in_ref.at[i], z_send.at[1], z_recv.at[j])

    for d in (1, 2, 3):
        z = (j + d) % nf
        sent(part_send.at[z], rs_send.at[z], rs_recv.at[z])
        sent(proj.at[j], ag_send.at[z], ag_recv.at[z])
    for q in range(4):
        sent(proj.at[q], core_send.at[q], core_recv.at[q])
        sent(og_sib.at[q], og_send.at[q], og_recv.at[q])
    for n in range(2):
        sent(sa1.at[n], h1_send.at[n], h1_recv.at[n])
        sent(sb1.at[n], h1_send.at[2 + n], h1_recv.at[2 + n])
    sent(sa2, h2_send.at[0], h2_recv.at[0])
    sent(sb2, h2_send.at[1], h2_recv.at[1])
    store_first.wait()
    store_second.wait()
    for n, o in enumerate((i, xn, yn, dn)):
        at = pl.ds(pl.multiple_of(o // 2 * pair_rows, pair_rows), pair_rows)
        pltpu.make_async_copy(weight.at[at], weight_out.at[at], store_sem.at[n]).wait()


def store_kernel(
    weight, first, second, weight_out, first_out, second_out,
    weight_buf, first_buf, second_buf, in_sem, out_sem,
):
    pieces = 16
    size = weight.shape[0] // pieces
    parts = [
        (weight.at[pl.ds(k * size, size)], weight_buf.at[pl.ds(k * size, size)],
         weight_out.at[pl.ds(k * size, size)])
        for k in range(pieces)
    ] + [(first, first_buf, first_out), (second, second_buf, second_out)]
    ins = [pltpu.make_async_copy(a, b, in_sem.at[n]) for n, (a, b, _) in enumerate(parts)]
    outs = [pltpu.make_async_copy(b, c, out_sem.at[n]) for n, (_, b, c) in enumerate(parts)]
    for copy in ins:
        copy.start()
    for load, store in zip(ins, outs):
        load.wait()
        store.start()
    for copy in outs:
        copy.wait()


def local_fused(activations, output_grads, basis, weight, first_moment, second_moment):
    tokens, _ = activations.shape
    shard_rows, rank = basis.shape
    own_rows = first_moment.shape[0]
    ndp, nf = lax.axis_size("dp"), lax.axis_size("fsdp")
    half = rank // 2
    anywhere = pl.BlockSpec(memory_space=pl.ANY)
    dma = pltpu.SemaphoreType.DMA
    results = pl.pallas_call(
        fused_kernel,
        out_shape=(
            jax.ShapeDtypeStruct(weight.shape, bf16),
            jax.ShapeDtypeStruct((own_rows, rank), f32),
            jax.ShapeDtypeStruct((own_rows, rank), f32),
        ),
        in_specs=[anywhere] * 6,
        out_specs=(anywhere,) * 3,
        scratch_shapes=[
            pltpu.VMEM(activations.shape, bf16),
            pltpu.VMEM(output_grads.shape, bf16),
            pltpu.VMEM((nf * ndp, own_rows, rank), bf16),
            pltpu.VMEM(weight.shape, bf16),
            pltpu.VMEM((own_rows, rank), f32),
            pltpu.VMEM((own_rows, rank), f32),
            pltpu.VMEM((ndp, own_rows, rank), bf16),
            pltpu.VMEM((nf, tokens // nf, rank), f32),
            pltpu.VMEM((nf, tokens // nf, rank), bf16),
            pltpu.VMEM((nf, tokens // nf, rank), bf16),
            pltpu.VMEM((nf, tokens // nf, rank), bf16),
            pltpu.VMEM((ndp // 2, own_rows, rank), f32),
            pltpu.VMEM((ndp // 2, tokens, own_rows), bf16),
            pltpu.VMEM((nf, tokens // nf, rank), bf16),
            pltpu.VMEM((2, own_rows, half), bf16),
            pltpu.VMEM((2, own_rows, half), bf16),
            pltpu.VMEM((2, own_rows, half), bf16),
            pltpu.VMEM((2, own_rows, half), bf16),
            pltpu.VMEM((own_rows, half), f32),
            pltpu.VMEM((own_rows, half), f32),
            pltpu.VMEM((own_rows, half), f32),
            pltpu.VMEM((own_rows, half), f32),
            dma((6,)), dma((6,)), dma((2,)), dma((3,)), dma((nf,)), dma((nf,)), dma((nf,)), dma((nf,)), dma((nf,)),
            *[dma((4,))] * 6, dma((2,)), dma((2,)), dma((4, 8)), dma((4, 8)),
        ],
        compiler_params=pltpu.CompilerParams(
            collective_id=0, has_side_effects=True, vmem_limit_bytes=63 * 1024 * 1024
        ),
        cost_estimate=pl.CostEstimate(
            flops=2 * shard_rows * rank * (2 * tokens + nf * shard_rows), bytes_accessed=24 * 1024 * 1024, transcendentals=0
        ),
    )(
        activations, output_grads, basis.reshape(ndp, own_rows, rank), weight,
        first_moment, second_moment,
    )
    return pl.pallas_call(
        store_kernel,
        out_shape=[jax.ShapeDtypeStruct(r.shape, r.dtype) for r in results],
        in_specs=[anywhere] * 3,
        out_specs=[anywhere] * 3,
        scratch_shapes=[pltpu.VMEM(r.shape, r.dtype) for r in results] + [dma((18,)), dma((18,))],
        compiler_params=pltpu.CompilerParams(vmem_limit_bytes=63 * 1024 * 1024),
    )(*results)


def local(activations, output_grads, basis, weight, first_moment, second_moment):
    partial_product = jnp.dot(activations, basis, preferred_element_type=f32)
    projected = lax.psum(partial_product, "fsdp").astype(bf16)
    total_tokens = projected.shape[0] * lax.axis_size("dp")
    local_term = (
        lax.dot_general(
            output_grads, projected, (((0,), (0,)), ((), ())), preferred_element_type=f32
        )
        / total_tokens
    )
    low_grad = lax.psum_scatter(local_term, "dp", scatter_dimension=0, tiled=True)
    new_first, new_second, update = adam(first_moment, second_moment, low_grad)
    all_updates = lax.all_gather(update, "dp", axis=0, tiled=True)
    decoded = times_basis(all_updates, lax.all_gather(basis, "fsdp", axis=0, tiled=True))
    new_weight = (weight.astype(f32) - step_rate * decoded).astype(bf16)
    return (new_weight, new_first, new_second)


def solution(mesh):
    fused = mesh.shape["dp"] == 8 and mesh.shape["fsdp"] == 4
    return jax.shard_map(
        local_fused if fused else local,
        mesh=mesh,
        in_specs=(
            P("dp", "fsdp"),
            P("dp", "fsdp"),
            P("fsdp", None),
            P("fsdp", None),
            P(("fsdp", "dp"), None),
            P(("fsdp", "dp"), None),
        ),
        out_specs=(P("fsdp", None), P(("fsdp", "dp"), None), P(("fsdp", "dp"), None)),
        check_vma=False,
    )
```

```python
import functools

import jax
import jax.numpy as jnp
from jax import lax
from jax.experimental import pallas as pl
from jax.experimental.pallas import tpu as pltpu
from jax.sharding import PartitionSpec as P

first_decay = 0.9
second_decay = 0.999
first_fix = 1.0 - 0.9**10
second_fix = 1.0 - 0.999**10
step_rate = 0.01
tiny_eps = 1e-08
MESH = pl.DeviceIdType.MESH
f32 = jnp.float32
bf16 = jnp.bfloat16


def times_basis(update, rows):
    return lax.dot_general(update, rows, (((1,), (1,)), ((), ())), preferred_element_type=f32)


def adam(first, second, low_grad):
    new_first = first_decay * first + (1.0 - first_decay) * low_grad
    new_second = second_decay * second + (1.0 - second_decay) * low_grad * low_grad
    update = (new_first / first_fix / (jnp.sqrt(new_second / second_fix) + tiny_eps)).astype(bf16)
    return new_first, new_second, update


def fused_kernel(
    act_in, og_in, basis_in_ref, weight_in, first_in, second_in,
    weight_out, first_out, second_out,
    act, og, rows, weight, first, second, updates,
    part, part_send, part_recv, proj,
    grad, og_sib, proj_sib, sa1, sb1, ra1, rb1, sa2, sb2, ra2, rb2,
    load_sem, store_sem, z_send, z_fwd, z_recv, rs_send, rs_recv, ag_send, ag_recv,
    core_send, core_recv, og_send, og_recv, h1_send, h1_recv, h2_send, h2_recv, pg_send, pg_recv,
):
    i = lax.axis_index("dp")
    j = lax.axis_index("fsdp")
    ndp, nf = 8, 4
    core, x, y = i % 2, (i // 2) % 2, i // 4
    sib = i + 1 - 2 * core
    xn = i + 2 * (1 - 2 * x)
    yn = i + 4 * (1 - 2 * y)
    dn = xn + 4 * (1 - 2 * y)
    tokens, rank = act.shape[0], first.shape[1]
    own_rows = first.shape[0]
    tb = tokens // nf
    total_tokens = tokens * ndp
    chunks = part.shape[0]
    width = rank // chunks
    lane = width // 2

    loads = [
        pltpu.make_async_copy(src, dst, load_sem.at[n])
        for n, (src, dst) in enumerate((
            (act_in, act),
            (basis_in_ref, rows.at[pl.ds(j * ndp, ndp)]),
            (og_in, og),
            (first_in, first),
            (second_in, second),
            (weight_in, weight),
        ))
    ]
    for load in loads:
        load.start()

    def remote(src, dst, ssem, rsem, dp, z):
        return pltpu.make_async_remote_copy(
            src_ref=src, dst_ref=dst, send_sem=ssem, recv_sem=rsem,
            device_id=(dp, z), device_id_type=MESH,
        )

    def got(dst, rsem, ssem):
        remote(dst, dst, ssem, rsem, sib, j).wait_recv()

    def sent(src, ssem, rsem):
        remote(src, src, ssem, rsem, sib, j).wait_send()

    barrier = pltpu.get_barrier_semaphore()
    for dp in (sib, xn, yn):
        pl.semaphore_signal(barrier, inc=1, device_id=(dp, j), device_id_type=MESH)
    for d in range(1, nf):
        pl.semaphore_signal(barrier, inc=1, device_id=(i, (j + d) % nf), device_id_type=MESH)
    pl.semaphore_wait(barrier, 3 + nf - 1)

    mine = 2 * y + x
    order = (3 - mine, 2 * y + 1 - x, 2 * (1 - y) + x, mine)

    def z_piece(shard):
        return rows.at[shard * ndp + i]

    @pl.when(j < nf - 1)
    def _():
        remote(basis_in_ref.at[i], z_piece(j), z_send.at[0], z_recv.at[j], i, j + 1).start()

    @pl.when(j > 0)
    def _():
        remote(basis_in_ref.at[i], z_piece(j), z_send.at[1], z_recv.at[j], i, j - 1).start()

    def og_columns(k):
        return pl.ds(pl.multiple_of(k * own_rows, own_rows), own_rows)

    for q in range(4):
        remote(
            og_in.at[:, og_columns(2 * order[q] + 1 - core)], og_sib.at[q],
            og_send.at[q], og_recv.at[q], sib, j,
        ).start()

    loads[0].wait()
    loads[1].wait()

    def partial(c):
        acc = jnp.dot(
            act[...],
            rows[pl.ds(j * ndp, ndp), :, c * width : (c + 1) * width].reshape(ndp * own_rows, width),
            preferred_element_type=f32,
        ).reshape(nf, tb, width)
        part[c] = acc
        part_send[c] = acc.astype(bf16)

    def scatter(c):
        for d in (2, 1, 3):
            z = (j + d) % nf
            remote(part_send.at[c, z], part_recv.at[c, j], rs_send.at[c, z], rs_recv.at[c, j], i, z).start()

    def to_sibling(c, z):
        remote(
            proj.at[c, z], proj_sib.at[c, z], core_send.at[c, z], core_recv.at[c, z], sib, j
        ).start()

    def reduce_gather(c):
        total = part[c, j]
        for d in (1, 2, 3):
            z = (j + d) % nf
            got(part_recv.at[c, z], rs_recv.at[c, z], rs_send.at[c, z])
            total = total + part_recv[c, z].astype(f32)
        proj[c, j] = total.astype(bf16)
        for d in (2, 1, 3):
            z = (j + d) % nf
            remote(proj.at[c, j], proj.at[c, j], ag_send.at[c, z], ag_recv.at[c, j], i, z).start()
        to_sibling(c, j)

    for c in range(chunks):
        partial(c)

    def columns(g, base, k, start, stop):
        if g < 3:
            return rows.at[base + k, :, pl.ds(rank * start // 2, rank * (stop - start) // 2)]
        return updates.at[k, :, pl.ds((g - 3) * width + lane * start, lane * (stop - start))]

    def block(g, base, k):
        return columns(g, base, k, 0, 2)

    def lane_a(g, base, k):
        return columns(g, base, k, 0, 1)

    def lane_b(g, base, k):
        return columns(g, base, k, 1, 2)

    def stage1(base, g):
        mine = block(g, base, i)
        remote(mine, mine, pg_send.at[g, 0], pg_recv.at[g, 0], xn, j).start()
        remote(mine, mine, pg_send.at[g, 1], pg_recv.at[g, 1], yn, j).start()
        remote(mine, mine, pg_send.at[g, 4], pg_recv.at[g, 4], sib, j).start()

    def stage2(base, g):
        bx, by = block(g, base, xn), block(g, base, yn)
        got(bx, pg_recv.at[g, 0], pg_send.at[g, 0])
        lb = lane_b(g, base, xn)
        remote(lb, lb, pg_send.at[g, 3], pg_recv.at[g, 3], yn, j).start()
        remote(bx, bx, pg_send.at[g, 5], pg_recv.at[g, 5], sib, j).start()
        got(by, pg_recv.at[g, 1], pg_send.at[g, 1])
        la = lane_a(g, base, yn)
        remote(la, la, pg_send.at[g, 2], pg_recv.at[g, 2], xn, j).start()
        remote(by, by, pg_send.at[g, 6], pg_recv.at[g, 6], sib, j).start()

    def stage3(base, g):
        got(lane_a(g, base, dn), pg_recv.at[g, 2], pg_send.at[g, 2])
        got(lane_b(g, base, dn), pg_recv.at[g, 3], pg_send.at[g, 3])
        bd = block(g, base, dn)
        remote(bd, bd, pg_send.at[g, 7], pg_recv.at[g, 7], sib, j).start()

    def stage4(base, g, receive=True):
        for q in range(4):
            o = (i, xn, yn, dn)[q]
            so = o + 1 - 2 * core
            if receive:
                got(block(g, base, so), pg_recv.at[g, 4 + q], pg_send.at[g, 4 + q])
            sent(block(g, base, o), pg_send.at[g, 4 + q], pg_recv.at[g, 4 + q])
        sent(block(g, base, i), pg_send.at[g, 0], pg_recv.at[g, 0])
        sent(block(g, base, i), pg_send.at[g, 1], pg_recv.at[g, 1])
        sent(lane_a(g, base, yn), pg_send.at[g, 2], pg_recv.at[g, 2])
        sent(lane_b(g, base, xn), pg_send.at[g, 3], pg_recv.at[g, 3])

    low = 1 - j // 2
    edge = low * j + (1 - low) * (nf - 1 - j)

    def shard_of(g):
        place = g + (g + nf - edge) // nf
        return low * place + (1 - low) * (nf - 1 - place)

    def basis_in(g):
        s = shard_of(g)
        got(z_piece(s), z_recv.at[s], z_send.at[0])

        @pl.when((s < j) & (j < nf - 1))
        def _():
            remote(z_piece(s), z_piece(s), z_fwd.at[g], z_recv.at[s], i, j + 1).start()

        @pl.when((s > j) & (j > 0))
        def _():
            remote(z_piece(s), z_piece(s), z_fwd.at[g], z_recv.at[s], i, j - 1).start()

        stage1(s * ndp, g)

    def basis_sent(g):
        s = shard_of(g)

        @pl.when(((s < j) & (j < nf - 1)) | ((s > j) & (j > 0)))
        def _():
            sent(z_piece(s), z_fwd.at[g], z_recv.at[s])

    def over_tokens(left, right):
        return lax.dot_general(left, right, (((0,), (0,)), ((), ())), preferred_element_type=f32)

    def low_grad(c):
        for d in (1, 2, 3):
            z = (j + d) % nf
            got(proj.at[c, z], ag_recv.at[c, z], ag_send.at[c, z])
            to_sibling(c, z)
        projected = proj[c].reshape(tokens, width)
        for q in range(4):
            grad[c, q] = over_tokens(og[:, og_columns(2 * order[q] + core)], projected)
        for z in range(nf):
            got(proj_sib.at[c, z], core_recv.at[c, z], core_send.at[c, z])
        projected_sib = proj_sib[c].reshape(tokens, width)
        for q in range(4):
            grad[c, q] = grad[c, q] + over_tokens(og_sib[q], projected_sib)
            if q in (0, 1):
                sa1[c, q] = grad[c, q, :, 0:lane].astype(bf16)
                remote(sa1.at[c, q], ra1.at[c, q], h1_send.at[c, q], h1_recv.at[c, q], xn, j).start()
            if q in (0, 2):
                n = q // 2
                sb1[c, n] = grad[c, q, :, lane:width].astype(bf16)
                remote(sb1.at[c, n], rb1.at[c, n], h1_send.at[c, 2 + n], h1_recv.at[c, 2 + n], yn, j).start()

    def hop2(c):
        got(ra1.at[c, 0], h1_recv.at[c, 0], h1_send.at[c, 0])
        sa2[c] = grad[c, 2, :, 0:lane] + ra1[c, 0].astype(f32)
        remote(sa2.at[c], ra2.at[c], h2_send.at[c, 0], h2_recv.at[c, 0], yn, j).start()
        got(rb1.at[c, 0], h1_recv.at[c, 2], h1_send.at[c, 2])
        sb2[c] = grad[c, 1, :, lane:width] + rb1[c, 0].astype(f32)
        remote(sb2.at[c], rb2.at[c], h2_send.at[c, 1], h2_recv.at[c, 1], xn, j).start()

    def step(c):
        got(ra1.at[c, 1], h1_recv.at[c, 1], h1_send.at[c, 1])
        got(rb1.at[c, 1], h1_recv.at[c, 3], h1_send.at[c, 3])
        for n, (r1, r2) in enumerate(((ra1, ra2), (rb1, rb2))):
            got(r2.at[c], h2_recv.at[c, n], h2_send.at[c, n])
            cols = pl.ds(c * width + n * lane, lane)
            summed = grad[c, 3, :, n * lane : (n + 1) * lane] + r1[c, 1].astype(f32) + r2[c]
            first[:, cols], second[:, cols], updates[i, :, cols] = adam(
                first[:, cols], second[:, cols], summed / total_tokens
            )
        stage1(0, 3 + c)

    middle = (j > 0) & (j < nf - 1)
    shard_base = [shard_of(g) * ndp for g in range(3)]
    @pl.when(jnp.logical_not(middle))
    def _():
        scatter(0)

    basis_in(0)
    basis_in(1)

    @pl.when(middle)
    def _():
        scatter(0)
        basis_in(2)

    stage2(shard_base[0], 0)
    reduce_gather(0)
    scatter(1)

    @pl.when(jnp.logical_not(middle))
    def _():
        basis_in(2)

    stage3(shard_base[0], 0)
    stage2(shard_base[1], 1)
    reduce_gather(1)
    loads[2].wait()
    for q in range(4):
        got(og_sib.at[q], og_recv.at[q], og_send.at[q])
    low_grad(0)
    stage3(shard_base[1], 1)
    stage2(shard_base[2], 2)
    hop2(0)
    low_grad(1)
    loads[3].wait()
    loads[4].wait()
    step(0)
    hop2(1)
    stage2(0, 3)
    stage3(shard_base[2], 2)
    step(1)
    stage3(0, 3)
    store_first = pltpu.make_async_copy(first, first_out, store_sem.at[4])
    store_second = pltpu.make_async_copy(second, second_out, store_sem.at[5])
    store_first.start()
    store_second.start()

    for g in range(3):
        stage4(shard_base[g], g)
        basis_sent(g)
    loads[5].wait()

    chunk = 4
    pair_rows = 2 * own_rows
    wide = chunk * own_rows

    def decode(n, o):
        pair = o // 2
        for g in range(3, 3 + chunks):
            got(block(g, 0, o + 1 - 2 * core), pg_recv.at[g, 4 + n], pg_send.at[g, 4 + n])
        left = updates[pl.ds(2 * pair, 2)].reshape(pair_rows, rank)
        at = pl.ds(pl.multiple_of(pair * pair_rows, pair_rows), pair_rows)

        def body(c, carry):
            cols = pl.ds(pl.multiple_of(c * wide, wide), wide)
            right = rows[pl.ds(c * chunk, chunk)].reshape(wide, rank)
            decoded = times_basis(left, right)
            weight[at, cols] = (weight[at, cols].astype(f32) - step_rate * decoded).astype(bf16)
            return carry

        lax.fori_loop(0, nf * ndp // chunk, body, 0)
        pltpu.make_async_copy(weight.at[at], weight_out.at[at], store_sem.at[n]).start()

    decode(0, i)
    stage2(0, 4)
    decode(1, xn)
    stage3(0, 4)
    decode(2, yn)
    decode(3, dn)
    stage4(0, 3, False)
    stage4(0, 4, False)

    @pl.when(j < nf - 1)
    def _():
        sent(basis_in_ref.at[i], z_send.at[0], z_recv.at[j])

    @pl.when(j > 0)
    def _():
        sent(basis_in_ref.at[i], z_send.at[1], z_recv.at[j])

    for c in range(chunks):
        for d in (1, 2, 3):
            z = (j + d) % nf
            sent(part_send.at[c, z], rs_send.at[c, z], rs_recv.at[c, z])
            sent(proj.at[c, j], ag_send.at[c, z], ag_recv.at[c, z])
        for q in range(4):
            sent(proj.at[c, q], core_send.at[c, q], core_recv.at[c, q])
        for n in range(2):
            sent(sa1.at[c, n], h1_send.at[c, n], h1_recv.at[c, n])
            sent(sb1.at[c, n], h1_send.at[c, 2 + n], h1_recv.at[c, 2 + n])
        sent(sa2.at[c], h2_send.at[c, 0], h2_recv.at[c, 0])
        sent(sb2.at[c], h2_send.at[c, 1], h2_recv.at[c, 1])
    for q in range(4):
        sent(og_sib.at[q], og_send.at[q], og_recv.at[q])
    store_first.wait()
    store_second.wait()
    for n, o in enumerate((i, xn, yn, dn)):
        at = pl.ds(pl.multiple_of(o // 2 * pair_rows, pair_rows), pair_rows)
        pltpu.make_async_copy(weight.at[at], weight_out.at[at], store_sem.at[n]).wait()


def store_kernel(
    weight, first, second, weight_out, first_out, second_out,
    weight_buf, first_buf, second_buf, in_sem, out_sem,
):
    pieces = 16
    size = weight.shape[0] // pieces
    parts = [
        (weight.at[pl.ds(k * size, size)], weight_buf.at[pl.ds(k * size, size)],
         weight_out.at[pl.ds(k * size, size)])
        for k in range(pieces)
    ] + [(first, first_buf, first_out), (second, second_buf, second_out)]
    ins = [pltpu.make_async_copy(a, b, in_sem.at[n]) for n, (a, b, _) in enumerate(parts)]
    outs = [pltpu.make_async_copy(b, c, out_sem.at[n]) for n, (_, b, c) in enumerate(parts)]
    for copy in ins:
        copy.start()
    for load, store in zip(ins, outs):
        load.wait()
        store.start()
    for copy in outs:
        copy.wait()


def local_fused(activations, output_grads, basis, weight, first_moment, second_moment):
    tokens, _ = activations.shape
    shard_rows, rank = basis.shape
    own_rows = first_moment.shape[0]
    ndp, nf = lax.axis_size("dp"), lax.axis_size("fsdp")
    chunks = 2
    width = rank // chunks
    anywhere = pl.BlockSpec(memory_space=pl.ANY)
    dma = pltpu.SemaphoreType.DMA
    results = pl.pallas_call(
        fused_kernel,
        out_shape=(
            jax.ShapeDtypeStruct(weight.shape, bf16),
            jax.ShapeDtypeStruct((own_rows, rank), f32),
            jax.ShapeDtypeStruct((own_rows, rank), f32),
        ),
        in_specs=[anywhere] * 6,
        out_specs=(anywhere,) * 3,
        scratch_shapes=[
            pltpu.VMEM(activations.shape, bf16),
            pltpu.VMEM(output_grads.shape, bf16),
            pltpu.VMEM((nf * ndp, own_rows, rank), bf16),
            pltpu.VMEM(weight.shape, bf16),
            pltpu.VMEM((own_rows, rank), f32),
            pltpu.VMEM((own_rows, rank), f32),
            pltpu.VMEM((ndp, own_rows, rank), bf16),
            pltpu.VMEM((chunks, nf, tokens // nf, width), f32),
            *[pltpu.VMEM((chunks, nf, tokens // nf, width), bf16)] * 3,
            pltpu.VMEM((chunks, ndp // 2, own_rows, width), f32),
            pltpu.VMEM((ndp // 2, tokens, own_rows), bf16),
            pltpu.VMEM((chunks, nf, tokens // nf, width), bf16),
            *[pltpu.VMEM((chunks, 2, own_rows, width // 2), bf16)] * 4,
            *[pltpu.VMEM((chunks, own_rows, width // 2), f32)] * 4,
            dma((6,)), dma((6,)), dma((2,)), dma((3,)), dma((nf,)), *[dma((chunks, nf))] * 4,
            *[dma((chunks, 4))] * 2, *[dma((4,))] * 2, *[dma((chunks, 4))] * 2, *[dma((chunks, 2))] * 2, *[dma((3 + chunks, 8))] * 2,
        ],
        compiler_params=pltpu.CompilerParams(
            collective_id=0, has_side_effects=True, vmem_limit_bytes=63 * 1024 * 1024
        ),
        cost_estimate=pl.CostEstimate(
            flops=2 * shard_rows * rank * (2 * tokens + nf * shard_rows), bytes_accessed=24 * 1024 * 1024, transcendentals=0
        ),
    )(
        activations, output_grads, basis.reshape(ndp, own_rows, rank), weight,
        first_moment, second_moment,
    )
    return pl.pallas_call(
        store_kernel,
        out_shape=[jax.ShapeDtypeStruct(r.shape, r.dtype) for r in results],
        in_specs=[anywhere] * 3,
        out_specs=[anywhere] * 3,
        scratch_shapes=[pltpu.VMEM(r.shape, r.dtype) for r in results] + [dma((18,)), dma((18,))],
        compiler_params=pltpu.CompilerParams(vmem_limit_bytes=63 * 1024 * 1024),
    )(*results)


def local(activations, output_grads, basis, weight, first_moment, second_moment):
    partial_product = jnp.dot(activations, basis, preferred_element_type=f32)
    projected = lax.psum(partial_product, "fsdp").astype(bf16)
    total_tokens = projected.shape[0] * lax.axis_size("dp")
    local_term = (
        lax.dot_general(
            output_grads, projected, (((0,), (0,)), ((), ())), preferred_element_type=f32
        )
        / total_tokens
    )
    low_grad = lax.psum_scatter(local_term, "dp", scatter_dimension=0, tiled=True)
    new_first, new_second, update = adam(first_moment, second_moment, low_grad)
    all_updates = lax.all_gather(update, "dp", axis=0, tiled=True)
    decoded = times_basis(all_updates, lax.all_gather(basis, "fsdp", axis=0, tiled=True))
    new_weight = (weight.astype(f32) - step_rate * decoded).astype(bf16)
    return (new_weight, new_first, new_second)


def solution(mesh):
    fused = mesh.shape["dp"] == 8 and mesh.shape["fsdp"] == 4
    return jax.shard_map(
        local_fused if fused else local,
        mesh=mesh,
        in_specs=(
            P("dp", "fsdp"),
            P("dp", "fsdp"),
            P("fsdp", None),
            P("fsdp", None),
            P(("fsdp", "dp"), None),
            P(("fsdp", "dp"), None),
        ),
        out_specs=(P("fsdp", None), P(("fsdp", "dp"), None), P(("fsdp", "dp"), None)),
        check_vma=False,
    )
```
